512 devices in a mesh: rel: 32 (over z, core), ent: 16 (over x, y).
Axes of the slice: x: 4, y: 4, z: 16, core: 2. Of those that a mesh axis runs over, the one named last changes fastest.
Arguments:
- anchors: bfloat16 [262144, 400], P(('rel', 'ent')), may hold values from -6 to 6
- rel_ids: int32 [262144, 1], P(('rel', 'ent')), may hold values from 0 to 511; in each aligned block of 512 rows (0 to 511, 512 to 1023, ...) at most 2 rows name the same one
- query_of: int32 [512, 512], P(('rel', 'ent')), may hold values from 0 to 255, never falling along the last dimension, each value on 1 to 3 neighbouring positions
- answer: int32 [131072], P(('rel', 'ent')), may hold values from 0 to 1023
- cand_ids: int32 [32, 1024], P('rel', 'ent'), may hold values from 0 to 4095, as said below
- ent_table: bfloat16 [4096, 400], P('ent'), may hold values from -6 to 6
- w_in: bfloat16 [512, 400, 1600], P(('rel', 'ent')), may hold values from -0.3125 to 0.3125
- w_out: bfloat16 [512, 1600, 400], P(('rel', 'ent')), may hold values from -0.15625 to 0.15625
- att_weight: bfloat16 [400, 400], replicated, may hold values from -0.3125 to 0.3125
Outputs:
- query_loss: float32 [131072], P(('rel', 'ent'))
- cand_grad: float32 [32, 1024, 400], P('rel', 'ent')
- w_in_grad: bfloat16 [512, 400, 1600], P(('rel', 'ent'))
The draws below stay inside these ranges and needn't reach their ends.
Inputs may be any that keep to these rules, and one draw needn't show every extreme that they name: `rel_ids`: among the branches of one device no relation occurs more than 2 times. `query_of`: A query's branches stand next to each other on its device; every query has 1 to 3 branches. `cand_ids`: for every group, ids b * 64 to (b + 1) * 64 - 1 of its list lie in table rows b * 256 to (b + 1) * 256 - 1.
All inputs are finite; a program needn't handle non-finite values.
Results may differ from the reference program's by a relative error of at most 0.017.
Values may be sent and summed in bfloat16 or wider, within the bound.
No kernel may reach another device: no remote copies, remote signals or barrier semaphores. Data moves between devices by JAX's collectives and lax.ppermute only.
A program may use at most 64 MiB of HBM per device.

```python
import math
import jax
import jax.numpy as jnp
import numpy as np
from jax import lax

D = 400
H = 1600
BR_DEV = 512
ENT_DEV = 256
NEG_DEV = 64
RELS = 512
CAP = 2
Q_DEV = 256
BRANCHES = 262144
QUERIES = 131072
GROUPS = 32
NEG = 1024
ENTITIES = 4096
N_REL = 32
N_ENT = 16


def draw_cand_ids(key, part):
    shards = NEG // NEG_DEV
    base = jax.random.randint(key, (GROUPS, shards, NEG_DEV), 0, ENT_DEV)
    offsets = jnp.arange(shards, dtype=jnp.int32)[None, :, None] * ENT_DEV
    ids_all = (base + offsets).reshape(GROUPS, NEG).astype(jnp.int32)
    low_spot = jax.random.randint(jax.random.fold_in(key, 11), (), 0, NEG_DEV)
    high_spot = jax.random.randint(jax.random.fold_in(key, 12), (), 0, NEG_DEV)
    ids_all = ids_all.at[0, low_spot].set(0)
    ids_all = ids_all.at[GROUPS - 1, (shards - 1) * NEG_DEV + high_spot].set(ENTITIES - 1)
    return ids_all


def plant(drawn, own_key, smallest, top_value):
    dims = drawn.shape
    place = [jax.random.randint(jax.random.fold_in(own_key, axis), (), 0, dims[axis]) for axis in range(len(dims))]
    drawn = drawn.at[tuple(place)].set(smallest)
    longest = dims.index(max(dims))
    place[longest] = (place[longest] + 1) % dims[longest]
    return drawn.at[tuple(place)].set(top_value)


def shard_levels(stream_key, extent, split, smallest, top_value):
    def one(dim, shards_of):
        steps = jax.random.uniform(jax.random.fold_in(jax.random.fold_in(stream_key, 6), dim), (shards_of,), jnp.float32, smallest / len(split), top_value / len(split))
        return jnp.repeat(jnp.exp(steps), extent[dim] // shards_of).reshape((-1,) + (1,) * (len(extent) - dim - 1))

    factor_of = one(*split[0])
    for cut in split[1:]:
        factor_of = factor_of * one(*cut)
    return factor_of


def length_profile(number_of, total, most, lean):
    weights = [(1 << 20) // math.isqrt(standing ** lean) + 1 for standing in range(2, number_of + 1)]
    rest, holding = total - most - (number_of - 1), [1] * (number_of - 1)
    while rest > 0:
        free = [i for i in range(number_of - 1) if holding[i] < most]
        whole, remaining = sum([weights[i] for i in free]), rest
        for i in free:
            more = min(most - holding[i], max(1, remaining * weights[i] // whole), rest)
            holding[i] = holding[i] + more
            rest = rest - more
    return np.array([most] + holding)


def ragged_sizes(stream_key, amount, total, bound, slope):
    if amount == 2:
        one = jax.random.randint(stream_key, (), max(1, total - bound), min(bound, total - 1) + 1)
        return jnp.stack([one, total - one])
    lengths = jnp.asarray(length_profile(amount, total, bound, slope), jnp.int32)
    couples = (amount - 1) // 2
    source_of, receiver = lengths[1:1 + 2 * couples:2], lengths[2:2 + 2 * couples:2]
    room = jnp.minimum(source_of - 1, bound - receiver)
    passed = jax.random.randint(jax.random.fold_in(stream_key, 1), (couples,), 0, 1 << 20) % (room + 1)
    lengths = lengths.at[1:1 + 2 * couples:2].set(source_of - passed).at[2:2 + 2 * couples:2].set(receiver + passed)
    return lengths[jax.random.permutation(jax.random.fold_in(stream_key, 2), amount)]


def deal_out(own_key, own, number, rows, amount, top, bound, slope):
    sequence = jax.random.permutation(own_key, amount)
    heavy_load, common = portions_of(amount, rows * top, bound, slope, True), portions_of(amount, rows * top, bound, slope, False)
    places = jnp.arange(amount)

    def named(lengths, rotation):
        used = int((lengths > 0).sum())
        fixed = max(1, used // 4)
        moved = fixed + (places - fixed + rotation * (used - fixed)) % max(1, amount - fixed)
        return jnp.zeros((amount,), jnp.int32).at[sequence[jnp.where(places < fixed, places, moved)]].set(jnp.asarray(lengths, jnp.int32))

    lengths = jnp.where(number % 4 == 0, named(heavy_load, number // 4), named(common, number - number // 4 - 1))
    mixed = jax.random.permutation(jax.random.fold_in(own, 3), amount)
    source_of, taker = mixed[0:amount // 2 * 2:2], mixed[1:amount // 2 * 2:2]
    margin = jnp.minimum(lengths[source_of] - 1, bound - lengths[taker]) // 2
    margin = jnp.where((source_of == sequence[0]) | (taker == sequence[0]) | (lengths[taker] == 0), 0, jnp.maximum(margin, 0))
    moved = jax.random.randint(jax.random.fold_in(own, 4), (amount // 2,), 0, 1 << 20) % (margin + 1)
    lengths = lengths.at[source_of].add(-moved).at[taker].add(moved)
    labels = jnp.searchsorted(jnp.cumsum(lengths), jnp.arange(rows * top), side="right").astype(jnp.int32)
    listing = labels.reshape(top, rows).T
    listing = listing[jax.random.permutation(jax.random.fold_in(own, 1), rows)]
    rotation = jax.random.randint(jax.random.fold_in(own, 2), (rows, 1), 0, top)
    return jnp.take_along_axis(listing, (jnp.arange(top)[None, :] + rotation) % top, axis=1)


def portions_of(count, total, reach, skew, full):
    portions = [(1 << 20) // math.isqrt(grade ** skew) + 1 for grade in range(1, count + 1)]
    largest = reach if full else min(reach, max(-(-total // count), total * portions[0] // sum(portions)))
    least = 1 if total - largest >= count - 1 else 0
    counts, spare = [largest] + [least] * (count - 1), total - largest - least * (count - 1)
    while spare > 0:
        free = [i for i in range(1, count) if counts[i] < largest] or [i for i in range(1, count) if counts[i] < reach]
        whole, budget = sum([portions[i] for i in free]), spare
        for i in free:
            addition = min(reach - counts[i], max(1, budget * portions[i] // whole), spare)
            counts[i] = counts[i] + addition
            spare = spare - addition
    return np.array(counts)


def normal_values(stream_key, shape, spread, bound, pieces=(), kind=jnp.bfloat16):
    entries = jax.random.normal(stream_key, shape, jnp.float32) * spread
    if len(pieces) > 0:
        entries = shard_levels(stream_key, shape, pieces, -0.22, 0.18) * entries
    return jnp.clip(entries, min=-bound, max=bound).astype(kind)


def setup_inputs(seed: int = 0) -> dict:
    streams_of = jax.random.split(jax.random.key(seed), 10)
    anchors = normal_values(streams_of[0], (BRANCHES, D), 1.0, 6.0, ((0, 512),))
    rel_ids_keys = jax.random.split(jax.random.fold_in(streams_of[1], 1), BRANCHES // BR_DEV)
    rel_ids_turns = jax.random.permutation(jax.random.fold_in(streams_of[1], 3), BRANCHES // BR_DEV)
    rel_ids = jax.vmap(lambda own, number: deal_out(jax.random.fold_in(streams_of[1], 2), own, number, BR_DEV, RELS, 1, CAP, 2))(rel_ids_keys, rel_ids_turns).reshape((BRANCHES, 1))
    query_of = jax.vmap(lambda own: jnp.searchsorted(jnp.cumsum(ragged_sizes(own, Q_DEV, BR_DEV, 3, 0)), jnp.arange(BR_DEV), side="right"))(jax.random.split(streams_of[2], (N_REL * N_ENT))).reshape((N_REL * N_ENT, BR_DEV)).astype(jnp.int32)
    answer = plant(jax.random.randint(streams_of[3], (QUERIES,), 0, NEG), jax.random.fold_in(streams_of[3], 1), 0, NEG - 1).astype(jnp.int32)
    cand_ids = draw_cand_ids(jax.random.fold_in(streams_of[9], 71), 0)
    ent_table = normal_values(streams_of[5], (ENTITIES, D), 1.0, 6.0, ((0, 16),))
    w_in = normal_values(streams_of[6], (RELS, D, H), D ** -0.5, 0.3125, ((0, 512),))
    w_out = normal_values(streams_of[7], (RELS, H, D), H ** -0.5, 0.15625, ((0, 512),))
    att_weight = normal_values(streams_of[8], (D, D), D ** -0.5, 0.3125)
    return {"anchors": anchors, "rel_ids": rel_ids, "query_of": query_of, "answer": answer, "cand_ids": cand_ids, "ent_table": ent_table, "w_in": w_in, "w_out": w_out, "att_weight": att_weight}


GELU_C = 0.7978845608
GELU_K = 0.044715
ATT_GAIN = 3.0


def gelu_pair(pre_act):
    inner_arg = GELU_C * (pre_act + GELU_K * pre_act * pre_act * pre_act)
    tangent = jnp.tanh(inner_arg)
    activated = 0.5 * pre_act * (1.0 + tangent)
    derivative = 0.5 * (1.0 + tangent) + 0.5 * pre_act * (1.0 - tangent * tangent) * GELU_C * (1.0 + 3.0 * GELU_K * pre_act * pre_act)
    return activated, derivative


def rank_in_device(relation_row):
    matches = relation_row[:, None] == relation_row[None, :]
    earlier = lax.broadcasted_iota(jnp.int32, matches.shape, 1) < lax.broadcasted_iota(jnp.int32, matches.shape, 0)
    return jnp.sum((matches & earlier).astype(jnp.int32), axis=1)


def reference(anchors, rel_ids, query_of, answer, cand_ids, ent_table, w_in, w_out, att_weight):
    owners = N_REL * N_ENT
    relation_grid = rel_ids[:, 0].reshape(owners, BR_DEV)
    position = lax.map(rank_in_device, relation_grid).reshape(-1)
    relation_flat = relation_grid.reshape(-1)
    source = jnp.repeat(jnp.arange(owners, dtype=jnp.int32), BR_DEV)
    inbox = jnp.zeros((RELS, owners, CAP, D), jnp.bfloat16).at[relation_flat, source, position].set(anchors)

    def forward_owner(operands):
        arrived, weight_in, weight_out = operands
        inputs = arrived.reshape(owners * CAP, D)
        hidden = gelu_pair(jnp.dot(inputs, weight_in, preferred_element_type=jnp.float32))[0].astype(jnp.bfloat16)
        moved = inputs.astype(jnp.float32) + jnp.dot(hidden, weight_out, preferred_element_type=jnp.float32)
        return moved.astype(jnp.bfloat16).reshape(owners, CAP, D)

    outbox = lax.map(forward_owner, (inbox, w_in, w_out))
    projected = outbox[relation_flat, source, position]
    proj_f = projected.astype(jnp.float32)
    att_tanh = jnp.tanh(jnp.dot(projected, att_weight, preferred_element_type=jnp.float32))
    att_exp = jnp.exp(ATT_GAIN * att_tanh)
    query_index = (query_of + jnp.arange(owners, dtype=jnp.int32)[:, None] * Q_DEV).reshape(-1)
    att_total = jax.ops.segment_sum(att_exp, query_index, num_segments=QUERIES)
    att_share = att_exp / att_total[query_index]
    query_f = jax.ops.segment_sum(att_share * proj_f, query_index, num_segments=QUERIES)
    query_b = query_f.astype(jnp.bfloat16)
    cand_rows = ent_table[cand_ids.reshape(-1)].reshape(GROUPS, NEG, D)
    score_scale = D ** -0.5

    def group_terms(operands):
        queries, candidates, correct = operands
        scores = jnp.dot(queries, candidates.T, preferred_element_type=jnp.float32) * score_scale
        is_answer = lax.broadcasted_iota(jnp.int32, scores.shape, 1) == correct[:, None]
        losses = jnp.sum(jnp.where(is_answer, jax.nn.softplus(-scores), jax.nn.softplus(scores) / (NEG - 1)), axis=1)
        coefficient = jnp.where(is_answer, -jax.nn.sigmoid(-scores), jax.nn.sigmoid(scores) / (NEG - 1)).astype(jnp.bfloat16)
        query_grad = jnp.dot(coefficient, candidates, preferred_element_type=jnp.float32) * score_scale
        rows_grad = jnp.dot(coefficient.T, queries, preferred_element_type=jnp.float32) * score_scale
        return losses, query_grad, rows_grad

    losses, query_grad, cand_grad = lax.map(group_terms, (query_b.reshape(GROUPS, N_ENT * Q_DEV, D), cand_rows, answer.reshape(GROUPS, N_ENT * Q_DEV)))
    query_loss = losses.reshape(QUERIES)
    grad_each = query_grad.reshape(QUERIES, D)[query_index]
    query_each = query_f[query_index]
    logit_grad = att_share * grad_each * (proj_f - query_each)
    pre_grad = (logit_grad * ATT_GAIN * (1.0 - att_tanh * att_tanh)).astype(jnp.bfloat16)
    proj_grad = (att_share * grad_each + jnp.dot(pre_grad, att_weight.T, preferred_element_type=jnp.float32)).astype(jnp.bfloat16)
    grad_box = jnp.zeros((RELS, owners, CAP, D), jnp.bfloat16).at[relation_flat, source, position].set(proj_grad)

    def backward_owner(operands):
        arrived, returned, weight_in, weight_out = operands
        inputs = arrived.reshape(owners * CAP, D)
        incoming = returned.reshape(owners * CAP, D)
        derivative = gelu_pair(jnp.dot(inputs, weight_in, preferred_element_type=jnp.float32))[1]
        hidden_grad = (jnp.dot(incoming, weight_out.T, preferred_element_type=jnp.float32) * derivative).astype(jnp.bfloat16)
        return jnp.dot(inputs.T, hidden_grad, preferred_element_type=jnp.float32).astype(jnp.bfloat16)

    w_in_grad = lax.map(backward_owner, (inbox, grad_box, w_in, w_out))
    return query_loss, cand_grad, w_in_grad
```

```python
import jax
import jax.numpy as jnp
from jax import lax
from jax.experimental import pallas as pl
from jax.experimental.pallas import tpu as pltpu
from jax.sharding import PartitionSpec as P

GELU_C = 0.7978845608
GELU_K = 0.044715
ATT_GAIN = 3.0
BOTH = ("rel", "ent")
F32 = jnp.float32
BF16 = jnp.bfloat16
VMEM_LIMIT = 56 * 1024 * 1024


def iota(shape, dim):
    return lax.broadcasted_iota(jnp.int32, shape, dim)


def mm(lhs, rhs, lhs_dim=1, rhs_dim=0):
    return lax.dot_general(
        lhs, rhs, (((lhs_dim,), (rhs_dim,)), ((), ())), preferred_element_type=F32
    )


def split(value):
    high = value.astype(BF16)
    return high, (value - high.astype(F32)).astype(BF16)


def call(kernel, outs, flops, moved, **more):
    return pl.pallas_call(
        kernel,
        out_shape=[jax.ShapeDtypeStruct(shape, dtype) for shape, dtype in outs],
        compiler_params=pltpu.CompilerParams(vmem_limit_bytes=VMEM_LIMIT),
        cost_estimate=pl.CostEstimate(flops=flops, bytes_accessed=moved, transcendentals=0),
        **more,
    )


def pack_kernel(rel_row, rel_col, anchors_t, packed, place):
    count = rel_row.shape[1]
    row = rel_row[...]
    same = (rel_col[...] == row) & (iota((count, count), 0) < iota((count, count), 1))
    rank = jnp.sum(jnp.where(same, 1.0, 0.0), axis=0, keepdims=True).astype(jnp.int32)
    slot = row * 2 + rank
    rows = packed.shape[0]
    step = 256
    for start in range(0, rows, step):
        hot = jnp.where(iota((step, count), 0) + start == slot, 1.0, 0.0).astype(BF16)
        place[start : start + step, :] = hot
        packed[start : start + step, :] = mm(hot, anchors_t[...], 1, 1).astype(BF16)


def maps_kernel(rel_row, rel_col, query_row, query_col, place_t, same_query, first, expand):
    count = rel_row.shape[1]
    queries = first.shape[0]
    col = rel_col[...]
    same = (col == rel_row[...]) & (iota((count, count), 1) < iota((count, count), 0))
    rank = jnp.sum(jnp.where(same, 1.0, 0.0), axis=1, keepdims=True).astype(jnp.int32)
    slot = col * 2 + rank
    place_t[...] = jnp.where(iota(place_t.shape, 1) == slot, 1.0, 0.0).astype(BF16)
    q_row = query_row[...]
    q_col = query_col[...]
    together = q_row == q_col
    same_query[...] = jnp.where(together, 1.0, 0.0).astype(BF16)
    earlier = together & (iota((count, count), 0) < iota((count, count), 1))
    before = jnp.sum(jnp.where(earlier, 1.0, 0.0), axis=0, keepdims=True)
    leading = jnp.where(before == 0.0, q_row, -1)
    first[...] = jnp.where(iota((queries, count), 0) == leading, 1.0, 0.0).astype(BF16)
    expand[...] = jnp.where(iota((count, queries), 1) == q_col, 1.0, 0.0).astype(BF16)


def gelu(pre):
    tangent = jnp.tanh(GELU_C * (pre + GELU_K * pre * pre * pre))
    return 0.5 * pre * (1.0 + tangent)


def gelu_slope(pre):
    square = pre * pre
    tangent = jnp.tanh(GELU_C * (pre + GELU_K * pre * square))
    return 0.5 * (1.0 + tangent) + 0.5 * pre * (1.0 - tangent * tangent) * GELU_C * (
        1.0 + 3.0 * GELU_K * square
    )


def forward_kernel(inputs, w_in, w_out_t, moved):
    rows = inputs[...]
    hidden = gelu(mm(rows, w_in[...])).astype(BF16)
    moved[...] = (rows.astype(F32) + mm(hidden, w_out_t[...], 1, 1)).astype(BF16)


def slope_kernel(inputs, w_in, slope):
    slope[...] = gelu_slope(mm(inputs[...], w_in[...])).astype(BF16)


def middle_kernel(
    returned,
    place_t,
    place,
    same_query,
    first,
    expand,
    att_weight,
    cands,
    answer,
    outgoing,
    coef_t,
    query_b,
    loss,
):
    width = returned.shape[1]
    scale = width ** (-0.5)
    projected = mm(place_t[...], returned[...])
    att_tanh = jnp.tanh(mm(projected.astype(BF16), att_weight[...]))
    att_exp = jnp.exp(ATT_GAIN * att_tanh)
    exp_hi, exp_lo = split(att_exp)
    both_hi, both_lo = split(att_exp * projected)
    group = same_query[...]
    inverse = 1.0 / (mm(group, exp_hi) + mm(group, exp_lo))
    query_each = (mm(group, both_hi) + mm(group, both_lo)) * inverse
    share = att_exp * inverse
    queries = mm(first[...], query_each.astype(BF16)).astype(BF16)
    query_b[...] = queries
    candidates = cands[:, :width]
    scores = mm(candidates, queries, 1, 1) * scale
    is_answer = iota(scores.shape, 0) == answer[...]
    signed = jnp.where(is_answer, -scores, scores)
    weight = jnp.where(is_answer, 1.0, 1.0 / (scores.shape[0] - 1))
    small = jnp.exp(-jnp.abs(signed))
    softplus = jnp.maximum(signed, 0.0) + jnp.log1p(small)
    loss[...] = jnp.sum(softplus * weight, axis=0, keepdims=True)
    sigmoid = jnp.where(signed >= 0.0, 1.0, small) / (1.0 + small) * weight
    coefficient = jnp.where(is_answer, -sigmoid, sigmoid).astype(BF16)
    coef_t[...] = coefficient
    grad_hi, grad_lo = split(mm(coefficient, candidates, 0, 0) * scale)
    spread = expand[...]
    grad_each = (mm(spread, grad_hi) + mm(spread, grad_lo)) * share
    pre_grad = grad_each * (projected - query_each) * ATT_GAIN * (1.0 - att_tanh * att_tanh)
    proj_grad = grad_each + mm(pre_grad.astype(BF16), att_weight[...], 1, 1)
    outgoing[...] = mm(place[...], proj_grad.astype(BF16)).astype(BF16)


def backward_kernel(incoming, inputs, slope, w_out_t, w_in_grad):
    hidden = w_in_grad.shape[1]
    grads = incoming[...]
    rows = inputs[...]
    step = 512
    for start in range(0, hidden, step):
        stop = min(start + step, hidden)
        part = mm(grads, w_out_t[:, start:stop])
        part = (part * slope[:, start:stop].astype(F32)).astype(BF16)
        w_in_grad[:, start:stop] = mm(rows, part, 0, 0).astype(BF16)


def shards(anchors, rel_ids, query_of, answer, cand_ids, ent_table, w_in, w_out, att_weight):
    owners = lax.axis_size("rel") * lax.axis_size("ent")
    branches, width = anchors.shape
    queries = answer.shape[0]
    slots = 2 * owners
    hidden = w_in.shape[2]
    weight_in = w_in[0]
    weight_out_t = w_out[0].T

    def exchange(rows):
        pairs = rows.reshape(owners, 2, width)
        pairs = lax.all_to_all(pairs, BOTH, split_axis=0, concat_axis=0, tiled=True)
        return pairs.reshape(slots, width)

    rel_row = rel_ids.reshape(1, branches)
    query_col = query_of.reshape(branches, 1)
    packed, place = call(
        pack_kernel,
        [((slots, width), BF16), ((slots, branches), BF16)],
        2 * slots * branches * width,
        4 * slots * branches,
    )(rel_row, rel_ids, anchors.T)
    inputs = exchange(packed)

    local_ids = cand_ids[0] - lax.axis_index("ent") * ent_table.shape[0]
    chosen = (local_ids[:, None] == iota((local_ids.shape[0], ent_table.shape[0]), 1)).astype(BF16)
    picked = jnp.dot(chosen, ent_table, preferred_element_type=F32).astype(BF16)
    picked = jnp.pad(picked, ((0, 0), (0, 512 - width)))
    cands = lax.all_gather(picked, "ent", axis=0, tiled=True)
    negatives = cands.shape[0]

    place_t, same_query, first, expand = call(
        maps_kernel,
        [
            ((branches, slots), BF16),
            ((branches, branches), BF16),
            ((queries, branches), BF16),
            ((branches, queries), BF16),
        ],
        10 * branches * slots,
        4 * branches * slots,
    )(rel_row, rel_ids, query_of, query_col)

    block = 256
    whole = lambda shape: pl.BlockSpec(shape, lambda i: (0, 0))
    rows_of = lambda cols: pl.BlockSpec((block, cols), lambda i: (i, 0))
    (moved,) = call(
        forward_kernel,
        [((slots, width), BF16)],
        4 * slots * width * hidden,
        4 * slots * width + 4 * width * hidden,
        grid=(slots // block,),
        in_specs=[rows_of(width), whole((width, hidden)), whole((width, hidden))],
        out_specs=[rows_of(width)],
    )(inputs, weight_in, weight_out_t)
    returned = exchange(moved)

    (slope,) = call(
        slope_kernel,
        [((slots, hidden), BF16)],
        2 * slots * width * hidden,
        2 * slots * hidden,
        grid=(slots // block,),
        in_specs=[rows_of(width), whole((width, hidden))],
        out_specs=[rows_of(hidden)],
    )(inputs, weight_in)

    outgoing, coef_t, query_b, loss = call(
        middle_kernel,
        [
            ((slots, width), BF16),
            ((negatives, queries), BF16),
            ((queries, width), BF16),
            ((1, queries), F32),
        ],
        4 * branches * slots * width,
        8 * slots * width,
    )(
        returned,
        place_t,
        place,
        same_query,
        first,
        expand,
        att_weight,
        cands,
        answer.reshape(1, queries),
    )
    incoming = exchange(outgoing)

    cand_part = jnp.dot(coef_t, query_b, preferred_element_type=F32) * width ** (-0.5)
    cand_grad = lax.psum_scatter(
        cand_part.astype(BF16), "ent", scatter_dimension=0, tiled=True
    ).astype(F32)

    (w_in_grad,) = call(
        backward_kernel,
        [((width, hidden), BF16)],
        4 * slots * width * hidden,
        4 * slots * hidden,
    )(incoming, inputs, slope, weight_out_t)
    return (loss.reshape(queries), cand_grad[None], w_in_grad[None])


def solution(mesh):
    placed = (
        P(BOTH, None),
        P(BOTH, None),
        P(BOTH, None),
        P(BOTH),
        P("rel", "ent"),
        P("ent", None),
        P(BOTH, None, None),
        P(BOTH, None, None),
        P(),
    )
    return jax.shard_map(
        shards,
        mesh=mesh,
        in_specs=placed,
        out_specs=(P(BOTH), P("rel", "ent", None), P(BOTH, None, None)),
        check_vma=False,
    )
```

```python
import jax
import jax.numpy as jnp
from jax import lax
from jax.experimental import pallas as pl
from jax.experimental.pallas import tpu as pltpu
from jax.sharding import PartitionSpec as P

GELU_C = 0.7978845608
GELU_K = 0.044715
ATT_GAIN = 3.0
BOTH = ("rel", "ent")
F32 = jnp.float32
BF16 = jnp.bfloat16
MIB = 1024 * 1024


def iota(shape, dim):
    return lax.broadcasted_iota(jnp.int32, shape, dim)


def mm(lhs, rhs, lhs_dim=1, rhs_dim=0):
    return lax.dot_general(
        lhs, rhs, (((lhs_dim,), (rhs_dim,)), ((), ())), preferred_element_type=F32
    )


def split(value):
    high = value.astype(BF16)
    return high, (value - high.astype(F32)).astype(BF16)


def call(kernel, outs, flops, moved, limit=16, **more):
    return pl.pallas_call(
        kernel,
        out_shape=[jax.ShapeDtypeStruct(shape, dtype) for shape, dtype in outs],
        compiler_params=pltpu.CompilerParams(vmem_limit_bytes=limit * MIB),
        cost_estimate=pl.CostEstimate(flops=flops, bytes_accessed=moved, transcendentals=0),
        **more,
    )


def pack_kernel(rel_row, rel_col, anchors_t, packed, place):
    count = rel_row.shape[1]
    row = rel_row[...]
    same = (rel_col[...] == row) & (iota((count, count), 0) < iota((count, count), 1))
    rank = jnp.sum(jnp.where(same, 1.0, 0.0), axis=0, keepdims=True).astype(jnp.int32)
    slot = row * 2 + rank
    rows = packed.shape[0]
    step = 256
    for start in range(0, rows, step):
        hot = jnp.where(iota((step, count), 0) + start == slot, 1.0, 0.0).astype(BF16)
        place[start : start + step, :] = hot
        packed[start : start + step, :] = mm(hot, anchors_t[...], 1, 1).astype(BF16)


def maps_kernel(rel_row, rel_col, query_row, query_col, place_t, same_query, first, expand):
    count = rel_row.shape[1]
    queries = first.shape[0]
    col = rel_col[...]
    same = (col == rel_row[...]) & (iota((count, count), 1) < iota((count, count), 0))
    rank = jnp.sum(jnp.where(same, 1.0, 0.0), axis=1, keepdims=True).astype(jnp.int32)
    slot = col * 2 + rank
    place_t[...] = jnp.where(iota(place_t.shape, 1) == slot, 1.0, 0.0).astype(BF16)
    q_row = query_row[...]
    q_col = query_col[...]
    together = q_row == q_col
    same_query[...] = jnp.where(together, 1.0, 0.0).astype(BF16)
    earlier = together & (iota((count, count), 0) < iota((count, count), 1))
    before = jnp.sum(jnp.where(earlier, 1.0, 0.0), axis=0, keepdims=True)
    leading = jnp.where(before == 0.0, q_row, -1)
    first[...] = jnp.where(iota((queries, count), 0) == leading, 1.0, 0.0).astype(BF16)
    expand[...] = jnp.where(iota((count, queries), 1) == q_col, 1.0, 0.0).astype(BF16)


def gelu(pre):
    tangent = jnp.tanh(GELU_C * (pre + GELU_K * pre * pre * pre))
    return 0.5 * pre * (1.0 + tangent)


def gelu_slope(pre):
    square = pre * pre
    tangent = jnp.tanh(GELU_C * (pre + GELU_K * pre * square))
    return 0.5 * (1.0 + tangent) + 0.5 * pre * (1.0 - tangent * tangent) * GELU_C * (
        1.0 + 3.0 * GELU_K * square
    )


def forward_kernel(inputs, w_in, w_out_t, moved):
    rows = inputs[...]
    total = rows.astype(F32)
    hidden = w_in.shape[1]
    for start in range(0, hidden, 512):
        stop = min(start + 512, hidden)
        active = gelu(mm(rows, w_in[:, start:stop])).astype(BF16)
        total = total + mm(active, w_out_t[:, start:stop], 1, 1)
    moved[...] = total.astype(BF16)


def slope_kernel(inputs, w_in, slope, inputs_t):
    rows = inputs[...]
    slope[...] = gelu_slope(mm(rows, w_in[...])).astype(BF16)
    inputs_t[...] = rows.T


def middle_kernel(
    returned,
    place_t,
    place,
    same_query,
    first,
    expand,
    att_weight,
    cands,
    answer,
    outgoing,
    coef_t,
    query_b,
    loss,
):
    width = returned.shape[1]
    scale = width ** (-0.5)
    projected = mm(place_t[...], returned[...])
    att_tanh = jnp.tanh(mm(projected.astype(BF16), att_weight[...]))
    att_exp = jnp.exp(ATT_GAIN * att_tanh)
    exp_hi, exp_lo = split(att_exp)
    both_hi, both_lo = split(att_exp * projected)
    group = same_query[...]
    inverse = 1.0 / (mm(group, exp_hi) + mm(group, exp_lo))
    query_each = (mm(group, both_hi) + mm(group, both_lo)) * inverse
    share = att_exp * inverse
    queries = mm(first[...], query_each.astype(BF16)).astype(BF16)
    query_b[...] = queries
    candidates = cands[:, :width]
    scores = mm(candidates, queries, 1, 1) * scale
    is_answer = iota(scores.shape, 0) == answer[...]
    signed = jnp.where(is_answer, -scores, scores)
    weight = jnp.where(is_answer, 1.0, 1.0 / (scores.shape[0] - 1))
    small = jnp.exp(-jnp.abs(signed))
    softplus = jnp.maximum(signed, 0.0) + jnp.log1p(small)
    loss[...] = jnp.sum(softplus * weight, axis=0, keepdims=True)
    sigmoid = jnp.where(signed >= 0.0, 1.0, small) / (1.0 + small) * weight
    coefficient = jnp.where(is_answer, -sigmoid, sigmoid).astype(BF16)
    coef_t[...] = coefficient
    grad_hi, grad_lo = split(mm(coefficient, candidates, 0, 0) * scale)
    spread = expand[...]
    grad_each = (mm(spread, grad_hi) + mm(spread, grad_lo)) * share
    pre_grad = grad_each * (projected - query_each) * ATT_GAIN * (1.0 - att_tanh * att_tanh)
    proj_grad = grad_each + mm(pre_grad.astype(BF16), att_weight[...], 1, 1)
    outgoing[...] = mm(place[...], proj_grad.astype(BF16)).astype(BF16)


def backward_kernel(incoming, inputs_t, slope, w_out_t, w_in_grad):
    hidden = w_in_grad.shape[1]
    grads = incoming[...]
    columns = inputs_t[...]
    step = 512
    for start in range(0, hidden, step):
        stop = min(start + step, hidden)
        part = mm(grads, w_out_t[:, start:stop])
        part = (part * slope[:, start:stop].astype(F32)).astype(BF16)
        w_in_grad[:, start:stop] = mm(columns, part).astype(BF16)


def scatter_sum(part, axis):
    count = lax.axis_size(axis)
    me = lax.axis_index(axis)
    gap = count // 2
    while gap:
        half = part.shape[0] // 2
        low, high = part[:half], part[half:]
        upper = (me & gap) != 0
        sent = jnp.where(upper, low, high)
        kept = jnp.where(upper, high, low)
        pairs = [(i, i ^ gap) for i in range(count)]
        got = lax.ppermute(sent.astype(BF16), axis, pairs)
        part = kept + got.astype(F32)
        gap //= 2
    return part


def shards(anchors, rel_ids, query_of, answer, cand_ids, ent_table, w_in, w_out, att_weight):
    owners = lax.axis_size("rel") * lax.axis_size("ent")
    branches, width = anchors.shape
    queries = answer.shape[0]
    slots = 2 * owners
    hidden = w_in.shape[2]
    weight_in = w_in[0]
    weight_out_t = w_out[0].T

    def exchange(rows):
        pairs = rows.reshape(owners, 2, width)
        pairs = lax.all_to_all(pairs, BOTH, split_axis=0, concat_axis=0, tiled=True)
        return pairs.reshape(slots, width)

    rel_row = rel_ids.reshape(1, branches)
    query_col = query_of.reshape(branches, 1)
    packed, place = call(
        pack_kernel,
        [((slots, width), BF16), ((slots, branches), BF16)],
        2 * slots * branches * width,
        4 * slots * branches,
    )(rel_row, rel_ids, anchors.T)
    inputs = exchange(packed)

    local_ids = cand_ids[0] - lax.axis_index("ent") * ent_table.shape[0]
    chosen = (local_ids[:, None] == iota((local_ids.shape[0], ent_table.shape[0]), 1)).astype(BF16)
    picked = jnp.dot(chosen, ent_table, preferred_element_type=F32).astype(BF16)
    picked = jnp.pad(picked, ((0, 0), (0, 512 - width)))
    cands = lax.all_gather(picked, "ent", axis=0, tiled=True)
    negatives = cands.shape[0]
    inputs, cands = lax.optimization_barrier((inputs, cands))

    place_t, same_query, first, expand = call(
        maps_kernel,
        [
            ((branches, slots), BF16),
            ((branches, branches), BF16),
            ((queries, branches), BF16),
            ((branches, queries), BF16),
        ],
        10 * branches * slots,
        4 * branches * slots,
    )(rel_row, rel_ids, query_of, query_col)

    block = 256
    whole = lambda shape: pl.BlockSpec(shape, lambda i: (0, 0))
    rows_of = lambda cols: pl.BlockSpec((block, cols), lambda i: (i, 0))
    (moved,) = call(
        forward_kernel,
        [((slots, width), BF16)],
        4 * slots * width * hidden,
        4 * slots * width + 4 * width * hidden,
        grid=(slots // block,),
        in_specs=[rows_of(width), whole((width, hidden)), whole((width, hidden))],
        out_specs=[rows_of(width)],
    )(inputs, weight_in, weight_out_t)
    returned = exchange(moved)

    slope, inputs_t = call(
        slope_kernel,
        [((slots, hidden), BF16), ((width, slots), BF16)],
        2 * slots * width * hidden,
        2 * slots * hidden,
        grid=(slots // block,),
        in_specs=[rows_of(width), whole((width, hidden))],
        out_specs=[rows_of(hidden), pl.BlockSpec((width, block), lambda i: (0, i))],
    )(inputs, weight_in)

    outgoing, coef_t, query_b, loss = call(
        middle_kernel,
        [
            ((slots, width), BF16),
            ((negatives, queries), BF16),
            ((queries, width), BF16),
            ((1, queries), F32),
        ],
        4 * branches * slots * width,
        8 * slots * width,
    )(
        returned,
        place_t,
        place,
        same_query,
        first,
        expand,
        att_weight,
        cands,
        answer.reshape(1, queries),
    )
    incoming = exchange(outgoing)

    cand_part = jnp.dot(coef_t, query_b, preferred_element_type=F32) * width ** (-0.5)
    cand_grad = scatter_sum(cand_part, "ent")

    (w_in_grad,) = call(
        backward_kernel,
        [((width, hidden), BF16)],
        4 * slots * width * hidden,
        4 * slots * hidden,
    )(incoming, inputs_t, slope, weight_out_t)
    return (loss.reshape(queries), cand_grad[None], w_in_grad[None])


def solution(mesh):
    placed = (
        P(BOTH, None),
        P(BOTH, None),
        P(BOTH, None),
        P(BOTH),
        P("rel", "ent"),
        P("ent", None),
        P(BOTH, None, None),
        P(BOTH, None, None),
        P(),
    )
    return jax.shard_map(
        shards,
        mesh=mesh,
        in_specs=placed,
        out_specs=(P(BOTH), P("rel", "ent", None), P(BOTH, None, None)),
        check_vma=False,
    )
```

```python
import jax
import jax.numpy as jnp
from jax import lax
from jax.experimental import pallas as pl
from jax.experimental.pallas import tpu as pltpu
from jax.sharding import PartitionSpec as P

GELU_C = 0.7978845608
GELU_K = 0.044715
ATT_GAIN = 3.0
BOTH = ("rel", "ent")
F32 = jnp.float32
BF16 = jnp.bfloat16
MIB = 1024 * 1024


def iota(shape, dim):
    return lax.broadcasted_iota(jnp.int32, shape, dim)


def mm(lhs, rhs, lhs_dim=1, rhs_dim=0):
    return lax.dot_general(
        lhs, rhs, (((lhs_dim,), (rhs_dim,)), ((), ())), preferred_element_type=F32
    )


def split(value):
    high = value.astype(BF16)
    return high, (value - high.astype(F32)).astype(BF16)


def call(kernel, outs, flops, moved, limit=56, **more):
    return pl.pallas_call(
        kernel,
        out_shape=[jax.ShapeDtypeStruct(shape, dtype) for shape, dtype in outs],
        compiler_params=pltpu.CompilerParams(vmem_limit_bytes=limit * MIB),
        cost_estimate=pl.CostEstimate(flops=flops, bytes_accessed=moved, transcendentals=0),
        **more,
    )


def pack_kernel(rel_row, rel_col, anchors_t, packed, place):
    count = rel_row.shape[1]
    row = rel_row[...]
    same = (rel_col[...] == row) & (iota((count, count), 0) < iota((count, count), 1))
    rank = jnp.sum(jnp.where(same, 1.0, 0.0), axis=0, keepdims=True).astype(jnp.int32)
    slot = row * 2 + rank
    rows = packed.shape[0]
    step = 256
    for start in range(0, rows, step):
        hot = jnp.where(iota((step, count), 0) + start == slot, 1.0, 0.0).astype(BF16)
        place[start : start + step, :] = hot
        packed[start : start + step, :] = mm(hot, anchors_t[...], 1, 1).astype(BF16)


def maps_kernel(rel_row, rel_col, query_row, query_col, place_t, same_query, first, expand):
    count = rel_row.shape[1]
    queries = first.shape[0]
    col = rel_col[...]
    same = (col == rel_row[...]) & (iota((count, count), 1) < iota((count, count), 0))
    rank = jnp.sum(jnp.where(same, 1.0, 0.0), axis=1, keepdims=True).astype(jnp.int32)
    slot = col * 2 + rank
    place_t[...] = jnp.where(iota(place_t.shape, 1) == slot, 1.0, 0.0).astype(BF16)
    q_row = query_row[...]
    q_col = query_col[...]
    together = q_row == q_col
    same_query[...] = jnp.where(together, 1.0, 0.0).astype(BF16)
    earlier = together & (iota((count, count), 0) < iota((count, count), 1))
    before = jnp.sum(jnp.where(earlier, 1.0, 0.0), axis=0, keepdims=True)
    leading = jnp.where(before == 0.0, q_row, -1)
    first[...] = jnp.where(iota((queries, count), 0) == leading, 1.0, 0.0).astype(BF16)
    expand[...] = jnp.where(iota((count, queries), 1) == q_col, 1.0, 0.0).astype(BF16)


def gelu(pre):
    tangent = jnp.tanh(GELU_C * (pre + GELU_K * pre * pre * pre))
    return 0.5 * pre * (1.0 + tangent)


def gelu_slope(pre):
    square = pre * pre
    tangent = jnp.tanh(GELU_C * (pre + GELU_K * pre * square))
    return 0.5 * (1.0 + tangent) + 0.5 * pre * (1.0 - tangent * tangent) * GELU_C * (
        1.0 + 3.0 * GELU_K * square
    )


def forward_kernel(inputs, w_in, w_out_t, moved):
    rows = inputs[...]
    total = rows.astype(F32)
    hidden = w_in.shape[1]
    for start in range(0, hidden, 512):
        stop = min(start + 512, hidden)
        active = gelu(mm(rows, w_in[:, start:stop])).astype(BF16)
        total = total + mm(active, w_out_t[:, start:stop], 1, 1)
    moved[...] = total.astype(BF16)


def slope_kernel(inputs, w_in, slope, inputs_t):
    rows = inputs[...]
    slope[...] = gelu_slope(mm(rows, w_in[...])).astype(BF16)
    inputs_t[...] = rows.T


def middle_kernel(
    returned,
    place_t,
    place,
    same_query,
    first,
    expand,
    att_weight,
    cands,
    answer,
    outgoing,
    coef_t,
    query_b,
    loss,
):
    width = returned.shape[1]
    scale = width ** (-0.5)
    projected = mm(place_t[...], returned[...])
    att_tanh = jnp.tanh(mm(projected.astype(BF16), att_weight[...]))
    att_exp = jnp.exp(ATT_GAIN * att_tanh)
    exp_hi, exp_lo = split(att_exp)
    both_hi, both_lo = split(att_exp * projected)
    group = same_query[...]
    inverse = 1.0 / (mm(group, exp_hi) + mm(group, exp_lo))
    query_each = (mm(group, both_hi) + mm(group, both_lo)) * inverse
    share = att_exp * inverse
    queries = mm(first[...], query_each.astype(BF16)).astype(BF16)
    query_b[...] = queries
    candidates = cands[:, :width]
    scores = mm(candidates, queries, 1, 1) * scale
    is_answer = iota(scores.shape, 0) == answer[...]
    signed = jnp.where(is_answer, -scores, scores)
    weight = jnp.where(is_answer, 1.0, 1.0 / (scores.shape[0] - 1))
    small = jnp.exp(-jnp.abs(signed))
    softplus = jnp.maximum(signed, 0.0) + jnp.log1p(small)
    loss[...] = jnp.sum(softplus * weight, axis=0, keepdims=True)
    sigmoid = jnp.where(signed >= 0.0, 1.0, small) / (1.0 + small) * weight
    coefficient = jnp.where(is_answer, -sigmoid, sigmoid).astype(BF16)
    coef_t[...] = coefficient
    grad_hi, grad_lo = split(mm(coefficient, candidates, 0, 0) * scale)
    spread = expand[...]
    grad_each = (mm(spread, grad_hi) + mm(spread, grad_lo)) * share
    pre_grad = grad_each * (projected - query_each) * ATT_GAIN * (1.0 - att_tanh * att_tanh)
    proj_grad = grad_each + mm(pre_grad.astype(BF16), att_weight[...], 1, 1)
    outgoing[...] = mm(place[...], proj_grad.astype(BF16)).astype(BF16)


def backward_kernel(incoming, inputs_t, slope, w_out_t, w_in_grad):
    hidden = w_in_grad.shape[1]
    grads = incoming[...]
    columns = inputs_t[...]
    step = 512
    for start in range(0, hidden, step):
        stop = min(start + step, hidden)
        part = mm(grads, w_out_t[:, start:stop])
        part = (part * slope[:, start:stop].astype(F32)).astype(BF16)
        w_in_grad[:, start:stop] = mm(columns, part).astype(BF16)


def scatter_sum(part, axis):
    count = lax.axis_size(axis)
    me = lax.axis_index(axis)
    gap = count // 2
    while gap:
        half = part.shape[0] // 2
        low, high = part[:half], part[half:]
        upper = (me & gap) != 0
        sent = jnp.where(upper, low, high)
        kept = jnp.where(upper, high, low)
        pairs = [(i, i ^ gap) for i in range(count)]
        got = lax.ppermute(sent.astype(BF16), axis, pairs)
        part = kept + got.astype(F32)
        gap //= 2
    return part


def shards(anchors, rel_ids, query_of, answer, cand_ids, ent_table, w_in, w_out, att_weight):
    owners = lax.axis_size("rel") * lax.axis_size("ent")
    branches, width = anchors.shape
    queries = answer.shape[0]
    slots = 2 * owners
    hidden = w_in.shape[2]
    weight_in = w_in[0]
    weight_out_t = w_out[0].T

    def exchange(rows):
        pairs = rows.reshape(owners, 2, width)
        pairs = lax.all_to_all(pairs, BOTH, split_axis=0, concat_axis=0, tiled=True)
        return pairs.reshape(slots, width)

    rel_row = rel_ids.reshape(1, branches)
    query_col = query_of.reshape(branches, 1)
    packed, place = call(
        pack_kernel,
        [((slots, width), BF16), ((slots, branches), BF16)],
        2 * slots * branches * width,
        4 * slots * branches,
    )(rel_row, rel_ids, anchors.T)
    inputs = exchange(packed)

    local_ids = cand_ids[0] - lax.axis_index("ent") * ent_table.shape[0]
    chosen = (local_ids[:, None] == iota((local_ids.shape[0], ent_table.shape[0]), 1)).astype(BF16)
    picked = jnp.dot(chosen, ent_table, preferred_element_type=F32).astype(BF16)
    picked = jnp.pad(picked, ((0, 0), (0, 512 - width)))
    cands = lax.all_gather(picked, "ent", axis=0, tiled=True)
    negatives = cands.shape[0]
    inputs, cands = lax.optimization_barrier((inputs, cands))

    place_t, same_query, first, expand = call(
        maps_kernel,
        [
            ((branches, slots), BF16),
            ((branches, branches), BF16),
            ((queries, branches), BF16),
            ((branches, queries), BF16),
        ],
        10 * branches * slots,
        4 * branches * slots,
    )(rel_row, rel_ids, query_of, query_col)

    block = 256
    whole = lambda shape: pl.BlockSpec(shape, lambda i: (0, 0))
    rows_of = lambda cols: pl.BlockSpec((block, cols), lambda i: (i, 0))
    (moved,) = call(
        forward_kernel,
        [((slots, width), BF16)],
        4 * slots * width * hidden,
        4 * slots * width + 4 * width * hidden,
        grid=(slots // block,),
        in_specs=[rows_of(width), whole((width, hidden)), whole((width, hidden))],
        out_specs=[rows_of(width)],
    )(inputs, weight_in, weight_out_t)
    returned = exchange(moved)

    slope, inputs_t = call(
        slope_kernel,
        [((slots, hidden), BF16), ((width, slots), BF16)],
        2 * slots * width * hidden,
        2 * slots * hidden,
        grid=(slots // block,),
        in_specs=[rows_of(width), whole((width, hidden))],
        out_specs=[rows_of(hidden), pl.BlockSpec((width, block), lambda i: (0, i))],
    )(inputs, weight_in)

    outgoing, coef_t, query_b, loss = call(
        middle_kernel,
        [
            ((slots, width), BF16),
            ((negatives, queries), BF16),
            ((queries, width), BF16),
            ((1, queries), F32),
        ],
        4 * branches * slots * width,
        8 * slots * width,
    )(
        returned,
        place_t,
        place,
        same_query,
        first,
        expand,
        att_weight,
        cands,
        answer.reshape(1, queries),
    )
    incoming = exchange(outgoing)

    cand_part = jnp.dot(coef_t, query_b, preferred_element_type=F32) * width ** (-0.5)
    cand_grad = scatter_sum(cand_part, "ent")

    (w_in_grad,) = call(
        backward_kernel,
        [((width, hidden), BF16)],
        4 * slots * width * hidden,
        4 * slots * hidden,
    )(incoming, inputs_t, slope, weight_out_t)
    return (loss.reshape(queries), cand_grad[None], w_in_grad[None])


def solution(mesh):
    placed = (
        P(BOTH, None),
        P(BOTH, None),
        P(BOTH, None),
        P(BOTH),
        P("rel", "ent"),
        P("ent", None),
        P(BOTH, None, None),
        P(BOTH, None, None),
        P(),
    )
    return jax.shard_map(
        shards,
        mesh=mesh,
        in_specs=placed,
        out_specs=(P(BOTH), P("rel", "ent", None), P(BOTH, None, None)),
        check_vma=False,
    )
```

```python
import jax
import jax.numpy as jnp
from jax import lax
from jax.experimental import pallas as pl
from jax.experimental.pallas import tpu as pltpu
from jax.sharding import PartitionSpec as P

GELU_C = 0.7978845608
GELU_K = 0.044715
ATT_GAIN = 3.0
BOTH = ("rel", "ent")
F32 = jnp.float32
BF16 = jnp.bfloat16
MIB = 1024 * 1024


def iota(shape, dim):
    return lax.broadcasted_iota(jnp.int32, shape, dim)


def mm(lhs, rhs, lhs_dim=1, rhs_dim=0):
    return lax.dot_general(
        lhs, rhs, (((lhs_dim,), (rhs_dim,)), ((), ())), preferred_element_type=F32
    )


def split(value):
    high = value.astype(BF16)
    return high, (value - high.astype(F32)).astype(BF16)


def call(kernel, outs, flops, moved, limit=56, **more):
    return pl.pallas_call(
        kernel,
        out_shape=[jax.ShapeDtypeStruct(shape, dtype) for shape, dtype in outs],
        compiler_params=pltpu.CompilerParams(vmem_limit_bytes=limit * MIB),
        cost_estimate=pl.CostEstimate(flops=flops, bytes_accessed=moved, transcendentals=0),
        **more,
    )


def fetch(sources, targets, sems):
    copies = [
        pltpu.make_async_copy(source, target, sems.at[number])
        for number, (source, target) in enumerate(zip(sources, targets))
    ]
    for copy in copies:
        copy.start()
    return copies


FAR = pl.BlockSpec(memory_space=pltpu.HBM)
NEAR = pl.BlockSpec(memory_space=pltpu.VMEM)


def room(arrays):
    return [pltpu.VMEM(a.shape, a.dtype) for a in arrays] + [
        pltpu.SemaphoreType.DMA((len(arrays),))
    ]


def pack_kernel(rel_row, rel_col, anchors_t, packed, place):
    count = rel_row.shape[1]
    row = rel_row[...]
    same = (rel_col[...] == row) & (iota((count, count), 0) < iota((count, count), 1))
    rank = jnp.sum(jnp.where(same, 1.0, 0.0), axis=0, keepdims=True).astype(jnp.int32)
    slot = row * 2 + rank
    rows = packed.shape[0]
    step = 256
    for start in range(0, rows, step):
        hot = jnp.where(iota((step, count), 0) + start == slot, 1.0, 0.0).astype(BF16)
        place[start : start + step, :] = hot
        packed[start : start + step, :] = mm(hot, anchors_t[...], 1, 1).astype(BF16)


def maps_kernel(rel_row, rel_col, query_row, query_col, place_t, same_query, first, expand):
    count = rel_row.shape[1]
    queries = first.shape[0]
    col = rel_col[...]
    same = (col == rel_row[...]) & (iota((count, count), 1) < iota((count, count), 0))
    rank = jnp.sum(jnp.where(same, 1.0, 0.0), axis=1, keepdims=True).astype(jnp.int32)
    slot = col * 2 + rank
    place_t[...] = jnp.where(iota(place_t.shape, 1) == slot, 1.0, 0.0).astype(BF16)
    q_row = query_row[...]
    q_col = query_col[...]
    together = q_row == q_col
    same_query[...] = jnp.where(together, 1.0, 0.0).astype(BF16)
    earlier = together & (iota((count, count), 0) < iota((count, count), 1))
    before = jnp.sum(jnp.where(earlier, 1.0, 0.0), axis=0, keepdims=True)
    leading = jnp.where(before == 0.0, q_row, -1)
    first[...] = jnp.where(iota((queries, count), 0) == leading, 1.0, 0.0).astype(BF16)
    expand[...] = jnp.where(iota((count, queries), 1) == q_col, 1.0, 0.0).astype(BF16)


def gelu(pre):
    tangent = jnp.tanh(GELU_C * (pre + GELU_K * pre * pre * pre))
    return 0.5 * pre * (1.0 + tangent)


def gelu_slope(pre):
    square = pre * pre
    tangent = jnp.tanh(GELU_C * (pre + GELU_K * pre * square))
    return 0.5 * (1.0 + tangent) + 0.5 * pre * (1.0 - tangent * tangent) * GELU_C * (
        1.0 + 3.0 * GELU_K * square
    )


def forward_kernel(inputs, w_in, w_out_t, moved):
    rows = inputs[...]
    hidden = gelu(mm(rows, w_in[...])).astype(BF16)
    moved[...] = (rows.astype(F32) + mm(hidden, w_out_t[...], 1, 1)).astype(BF16)


def slope_kernel(inputs, w_in, slope, inputs_t):
    rows = inputs[...]
    slope[...] = gelu_slope(mm(rows, w_in[...])).astype(BF16)
    inputs_t[...] = rows.T


def middle_kernel(
    returned,
    answer,
    far_place_t,
    far_weight,
    far_same,
    far_first,
    far_cands,
    far_expand,
    far_place,
    outgoing,
    coef_t,
    query_b,
    loss,
    place_t,
    att_weight,
    same_query,
    first,
    cands,
    expand,
    place,
    sems,
):
    copies = fetch(
        (far_place_t, far_weight, far_same, far_first, far_cands, far_expand, far_place),
        (place_t, att_weight, same_query, first, cands, expand, place),
        sems,
    )
    width = returned.shape[1]
    scale = width ** (-0.5)
    copies[0].wait()
    projected = mm(place_t[...], returned[...])
    copies[1].wait()
    att_tanh = jnp.tanh(mm(projected.astype(BF16), att_weight[...]))
    att_exp = jnp.exp(ATT_GAIN * att_tanh)
    exp_hi, exp_lo = split(att_exp)
    both_hi, both_lo = split(att_exp * projected)
    copies[2].wait()
    group = same_query[...]
    inverse = 1.0 / (mm(group, exp_hi) + mm(group, exp_lo))
    query_each = (mm(group, both_hi) + mm(group, both_lo)) * inverse
    share = att_exp * inverse
    copies[3].wait()
    queries = mm(first[...], query_each.astype(BF16)).astype(BF16)
    query_b[...] = queries
    copies[4].wait()
    candidates = cands[...]
    scores = mm(candidates, queries, 1, 1) * scale
    is_answer = iota(scores.shape, 0) == answer[...]
    signed = jnp.where(is_answer, -scores, scores)
    weight = jnp.where(is_answer, 1.0, 1.0 / (scores.shape[0] - 1))
    small = jnp.exp(-jnp.abs(signed))
    softplus = jnp.maximum(signed, 0.0) + jnp.log1p(small)
    loss[...] = jnp.sum(softplus * weight, axis=0, keepdims=True)
    sigmoid = jnp.where(signed >= 0.0, 1.0, small) / (1.0 + small) * weight
    coefficient = jnp.where(is_answer, -sigmoid, sigmoid).astype(BF16)
    coef_t[...] = coefficient
    grad_hi, grad_lo = split(mm(coefficient, candidates, 0, 0) * scale)
    copies[5].wait()
    spread = expand[...]
    grad_each = (mm(spread, grad_hi) + mm(spread, grad_lo)) * share
    pre_grad = grad_each * (projected - query_each) * ATT_GAIN * (1.0 - att_tanh * att_tanh)
    proj_grad = grad_each + mm(pre_grad.astype(BF16), att_weight[...], 1, 1)
    copies[6].wait()
    outgoing[...] = mm(place[...], proj_grad.astype(BF16)).astype(BF16)


def backward_kernel(incoming, w_out_t, slope, inputs_t, w_in_grad):
    part = (mm(incoming[...], w_out_t[...]) * slope[...].astype(F32)).astype(BF16)
    w_in_grad[...] = mm(inputs_t[...], part).astype(BF16)


def scatter_sum(part, axis):
    count = lax.axis_size(axis)
    me = lax.axis_index(axis)
    gap = count // 2
    while gap:
        half = part.shape[0] // 2
        low, high = part[:half], part[half:]
        upper = (me & gap) != 0
        sent = jnp.where(upper, low, high)
        kept = jnp.where(upper, high, low)
        pairs = [(i, i ^ gap) for i in range(count)]
        got = lax.ppermute(sent.astype(BF16), axis, pairs)
        part = kept + got.astype(F32)
        gap //= 2
    return part


def shards(anchors, rel_ids, query_of, answer, cand_ids, ent_table, w_in, w_out, att_weight):
    owners = lax.axis_size("rel") * lax.axis_size("ent")
    branches, width = anchors.shape
    queries = answer.shape[0]
    slots = 2 * owners
    hidden = w_in.shape[2]
    weight_in = w_in[0]
    weight_out_t = w_out[0].T

    def exchange(rows):
        pairs = rows.reshape(owners, 2, width)
        pairs = lax.all_to_all(pairs, BOTH, split_axis=0, concat_axis=0, tiled=True)
        return pairs.reshape(slots, width)

    rel_row = rel_ids.reshape(1, branches)
    query_col = query_of.reshape(branches, 1)
    packed, place = call(
        pack_kernel,
        [((slots, width), BF16), ((slots, branches), BF16)],
        2 * slots * branches * width,
        4 * slots * branches,
        limit=16,
    )(rel_row, rel_ids, anchors.T)
    inputs = exchange(packed)

    local_ids = cand_ids[0] - lax.axis_index("ent") * ent_table.shape[0]
    chosen = (local_ids[:, None] == iota((local_ids.shape[0], ent_table.shape[0]), 1)).astype(BF16)
    picked = jnp.dot(chosen, ent_table, preferred_element_type=F32).astype(BF16)
    cands = lax.all_gather(picked, "ent", axis=0, tiled=True)
    negatives = cands.shape[0]
    inputs, cands = lax.optimization_barrier((inputs, cands))

    place_t, same_query, first, expand = call(
        maps_kernel,
        [
            ((branches, slots), BF16),
            ((branches, branches), BF16),
            ((queries, branches), BF16),
            ((branches, queries), BF16),
        ],
        10 * branches * slots,
        4 * branches * slots,
    )(rel_row, rel_ids, query_of, query_col)

    block = 256
    half = slots // 2
    columns = 896
    whole = lambda shape: pl.BlockSpec(shape, lambda i: (0, 0))
    rows_of = lambda cols: pl.BlockSpec((block, cols), lambda i: (i, 0))
    (moved,) = call(
        forward_kernel,
        [((slots, width), BF16)],
        4 * slots * width * hidden,
        4 * slots * width + 4 * width * hidden,
        grid=(slots // half,),
        in_specs=[
            pl.BlockSpec((half, width), lambda i: (i, 0)),
            whole((width, hidden)),
            whole((width, hidden)),
        ],
        out_specs=[pl.BlockSpec((half, width), lambda i: (i, 0))],
    )(inputs, weight_in, weight_out_t)
    returned = exchange(moved)

    slope, inputs_t = call(
        slope_kernel,
        [((slots, hidden), BF16), ((width, slots), BF16)],
        2 * slots * width * hidden,
        2 * slots * hidden,
        grid=(slots // block,),
        in_specs=[rows_of(width), whole((width, hidden))],
        out_specs=[rows_of(hidden), pl.BlockSpec((width, block), lambda i: (0, i))],
    )(inputs, weight_in)

    far = (place_t, att_weight, same_query, first, cands, expand, place)
    outgoing, coef_t, query_b, loss = call(
        middle_kernel,
        [
            ((slots, width), BF16),
            ((negatives, queries), BF16),
            ((queries, width), BF16),
            ((1, queries), F32),
        ],
        4 * branches * slots * width,
        8 * slots * width,
        in_specs=[NEAR, NEAR] + [FAR] * len(far),
        out_specs=[NEAR] * 4,
        scratch_shapes=room(far),
    )(returned, answer.reshape(1, queries), *far)
    incoming = exchange(outgoing)

    cand_part = jnp.dot(coef_t, query_b, preferred_element_type=F32) * width ** (-0.5)
    cand_grad = scatter_sum(cand_part, "ent")

    (w_in_grad,) = call(
        backward_kernel,
        [((width, hidden), BF16)],
        4 * slots * width * hidden,
        4 * slots * hidden,
        grid=(pl.cdiv(hidden, columns),),
        in_specs=[
            whole((slots, width)),
            pl.BlockSpec((width, columns), lambda i: (0, i)),
            pl.BlockSpec((slots, columns), lambda i: (0, i)),
            whole((width, slots)),
        ],
        out_specs=[pl.BlockSpec((width, columns), lambda i: (0, i))],
    )(incoming, weight_out_t, slope, inputs_t)
    return (loss.reshape(queries), cand_grad[None], w_in_grad[None])


def solution(mesh):
    placed = (
        P(BOTH, None),
        P(BOTH, None),
        P(BOTH, None),
        P(BOTH),
        P("rel", "ent"),
        P("ent", None),
        P(BOTH, None, None),
        P(BOTH, None, None),
        P(),
    )
    return jax.shard_map(
        shards,
        mesh=mesh,
        in_specs=placed,
        out_specs=(P(BOTH), P("rel", "ent", None), P(BOTH, None, None)),
        check_vma=False,
    )
```

```python
import jax
import jax.numpy as jnp
from jax import lax
from jax.experimental import pallas as pl
from jax.experimental.pallas import tpu as pltpu
from jax.sharding import PartitionSpec as P

GELU_C = 0.7978845608
GELU_K = 0.044715
ATT_GAIN = 3.0
BOTH = ("rel", "ent")
F32 = jnp.float32
BF16 = jnp.bfloat16
MIB = 1024 * 1024


def iota(shape, dim):
    return lax.broadcasted_iota(jnp.int32, shape, dim)


def mm(lhs, rhs, lhs_dim=1, rhs_dim=0):
    return lax.dot_general(
        lhs, rhs, (((lhs_dim,), (rhs_dim,)), ((), ())), preferred_element_type=F32
    )


def split(value):
    high = value.astype(BF16)
    return high, (value - high.astype(F32)).astype(BF16)


def call(kernel, outs, flops, moved, limit=56, **more):
    return pl.pallas_call(
        kernel,
        out_shape=[jax.ShapeDtypeStruct(shape, dtype) for shape, dtype in outs],
        compiler_params=pltpu.CompilerParams(vmem_limit_bytes=limit * MIB),
        cost_estimate=pl.CostEstimate(flops=flops, bytes_accessed=moved, transcendentals=0),
        **more,
    )


def fetch(sources, targets, sems):
    copies = [
        pltpu.make_async_copy(source, target, sems.at[number])
        for number, (source, target) in enumerate(zip(sources, targets))
    ]
    for copy in copies:
        copy.start()
    return copies


FAR = pl.BlockSpec(memory_space=pltpu.HBM)
NEAR = pl.BlockSpec(memory_space=pltpu.VMEM)


def room(arrays):
    return [pltpu.VMEM(a.shape, a.dtype) for a in arrays] + [
        pltpu.SemaphoreType.DMA((len(arrays),))
    ]


def pack_kernel(rel_row, rel_col, anchors_t, packed):
    count = rel_row.shape[1]
    row = rel_row[...]
    same = (rel_col[...] == row) & (iota((count, count), 0) < iota((count, count), 1))
    rank = jnp.sum(jnp.where(same, 1.0, 0.0), axis=0, keepdims=True).astype(jnp.int32)
    slot = row * 2 + rank
    rows = packed.shape[0]
    step = 256
    for start in range(0, rows, step):
        hot = jnp.where(iota((step, count), 0) + start == slot, 1.0, 0.0).astype(BF16)
        packed[start : start + step, :] = mm(hot, anchors_t[...], 1, 1).astype(BF16)


def maps_kernel(
    rel_row, rel_col, query_row, query_col, place, place_t, same_query, first, expand
):
    count = rel_row.shape[1]
    queries = first.shape[0]
    col = rel_col[...]
    row = rel_row[...]
    below = iota((count, count), 0) < iota((count, count), 1)
    above = iota((count, count), 0) > iota((count, count), 1)
    equal = col == row
    rank = jnp.sum(jnp.where(equal & below, 1.0, 0.0), axis=0, keepdims=True)
    slot = row * 2 + rank.astype(jnp.int32)
    place[...] = jnp.where(iota(place.shape, 0) == slot, 1.0, 0.0).astype(BF16)
    rank = jnp.sum(jnp.where(equal & above, 1.0, 0.0), axis=1, keepdims=True)
    slot = col * 2 + rank.astype(jnp.int32)
    place_t[...] = jnp.where(iota(place_t.shape, 1) == slot, 1.0, 0.0).astype(BF16)
    q_row = query_row[...]
    q_col = query_col[...]
    together = q_row == q_col
    same_query[...] = jnp.where(together, 1.0, 0.0).astype(BF16)
    before = jnp.sum(jnp.where(together & below, 1.0, 0.0), axis=0, keepdims=True)
    leading = jnp.where(before == 0.0, q_row, -1)
    first[...] = jnp.where(iota((queries, count), 0) == leading, 1.0, 0.0).astype(BF16)
    expand[...] = jnp.where(iota((count, queries), 1) == q_col, 1.0, 0.0).astype(BF16)


def gelu(pre):
    tangent = jnp.tanh(GELU_C * (pre + GELU_K * pre * pre * pre))
    return 0.5 * pre * (1.0 + tangent)


def gelu_slope(pre):
    square = pre * pre
    tangent = jnp.tanh(GELU_C * (pre + GELU_K * pre * square))
    return 0.5 * (1.0 + tangent) + 0.5 * pre * (1.0 - tangent * tangent) * GELU_C * (
        1.0 + 3.0 * GELU_K * square
    )


def forward_kernel(inputs, w_in, w_out_t, moved):
    rows = inputs[...]
    hidden = gelu(mm(rows, w_in[...])).astype(BF16)
    moved[...] = (rows.astype(F32) + mm(hidden, w_out_t[...], 1, 1)).astype(BF16)


def slope_kernel(inputs, w_in, slope, inputs_t):
    rows = inputs[...]
    slope[...] = gelu_slope(mm(rows, w_in[...])).astype(BF16)
    inputs_t[...] = rows.T


def sigmoid_parts(scores, is_answer, negatives):
    signed = jnp.where(is_answer, -scores, scores)
    small = jnp.exp(-jnp.abs(signed))
    weight = jnp.where(is_answer, -1.0, 1.0 / (negatives - 1))
    sigmoid = jnp.where(signed >= 0.0, 1.0, small) / (1.0 + small)
    return signed, small, (sigmoid * weight).astype(BF16)


def middle_kernel(
    answer,
    far_returned,
    far_place_t,
    far_weight,
    far_same,
    far_first,
    far_cands,
    far_expand,
    far_place,
    outgoing,
    query_b,
    returned,
    place_t,
    att_weight,
    same_query,
    first,
    cands,
    expand,
    place,
    sems,
):
    copies = fetch(
        (
            far_returned,
            far_place_t,
            far_weight,
            far_same,
            far_first,
            far_cands,
            far_expand,
            far_place,
        ),
        (returned, place_t, att_weight, same_query, first, cands, expand, place),
        sems,
    )
    scale = returned.shape[1] ** (-0.5)
    copies[0].wait()
    copies[1].wait()
    projected = mm(place_t[...], returned[...])
    copies[2].wait()
    att_tanh = jnp.tanh(mm(projected.astype(BF16), att_weight[...]))
    att_exp = jnp.exp(ATT_GAIN * att_tanh)
    exp_hi, exp_lo = split(att_exp)
    both_hi, both_lo = split(att_exp * projected)
    copies[3].wait()
    group = same_query[...]
    inverse = 1.0 / (mm(group, exp_hi) + mm(group, exp_lo))
    query_each = (mm(group, both_hi) + mm(group, both_lo)) * inverse
    share = att_exp * inverse
    copies[4].wait()
    queries = mm(first[...], query_each.astype(BF16)).astype(BF16)
    query_b[...] = queries
    copies[5].wait()
    scores = mm(queries, cands[...], 1, 1) * scale
    is_answer = iota(scores.shape, 1) == answer[...]
    _, _, coefficient = sigmoid_parts(scores, is_answer, scores.shape[1])
    grad_hi, grad_lo = split(mm(coefficient, cands[...]) * scale)
    copies[6].wait()
    spread = expand[...]
    grad_each = (mm(spread, grad_hi) + mm(spread, grad_lo)) * share
    pre_grad = grad_each * (projected - query_each) * ATT_GAIN * (1.0 - att_tanh * att_tanh)
    proj_grad = grad_each + mm(pre_grad.astype(BF16), att_weight[...], 1, 1)
    copies[7].wait()
    outgoing[...] = mm(place[...], proj_grad.astype(BF16)).astype(BF16)


def loss_kernel(cands, query_b, answer, loss, cand_part):
    negatives, width = cands.shape
    scale = width ** (-0.5)
    queries = query_b[...]
    scores = mm(cands[...], queries, 1, 1) * scale
    is_answer = iota(scores.shape, 0) == answer[...]
    signed, small, coefficient = sigmoid_parts(scores, is_answer, negatives)
    softplus = jnp.maximum(signed, 0.0) + jnp.log1p(small)
    weight = jnp.where(is_answer, 1.0, 1.0 / (negatives - 1))
    loss[...] = jnp.sum(softplus * weight, axis=0, keepdims=True)
    cand_part[...] = mm(coefficient, queries) * scale


def backward_kernel(incoming, w_out_t, slope, inputs_t, w_in_grad):
    part = (mm(incoming[...], w_out_t[...]) * slope[...].astype(F32)).astype(BF16)
    w_in_grad[...] = mm(inputs_t[...], part).astype(BF16)


def scatter_sum(part, axis):
    count = lax.axis_size(axis)
    me = lax.axis_index(axis)
    gap = count // 2
    while gap:
        half = part.shape[0] // 2
        low, high = part[:half], part[half:]
        upper = (me & gap) != 0
        sent = jnp.where(upper, low, high)
        kept = jnp.where(upper, high, low)
        pairs = [(i, i ^ gap) for i in range(count)]
        got = lax.ppermute(sent.astype(BF16), axis, pairs)
        part = kept + got.astype(F32)
        gap //= 2
    return part


def shards(anchors, rel_ids, query_of, answer, cand_ids, ent_table, w_in, w_out, att_weight):
    owners = lax.axis_size("rel") * lax.axis_size("ent")
    branches, width = anchors.shape
    queries = answer.shape[0]
    slots = 2 * owners
    hidden = w_in.shape[2]
    weight_in = w_in[0]
    weight_out_t = w_out[0].T

    def exchange(rows):
        pairs = rows.reshape(owners, 2, width)
        pairs = lax.all_to_all(pairs, BOTH, split_axis=0, concat_axis=0, tiled=True)
        return pairs.reshape(slots, width)

    rel_row = rel_ids.reshape(1, branches)
    query_col = query_of.reshape(branches, 1)
    (packed,) = call(
        pack_kernel,
        [((slots, width), BF16)],
        2 * slots * branches * width,
        4 * slots * branches,
        limit=16,
    )(rel_row, rel_ids, anchors.T)
    inputs = exchange(packed)

    local_ids = cand_ids[0] - lax.axis_index("ent") * ent_table.shape[0]
    chosen = (local_ids[:, None] == iota((local_ids.shape[0], ent_table.shape[0]), 1)).astype(BF16)
    picked = jnp.dot(chosen, ent_table, preferred_element_type=F32).astype(BF16)
    cands = lax.all_gather(picked, "ent", axis=0, tiled=True)
    negatives = cands.shape[0]
    inputs, cands = lax.optimization_barrier((inputs, cands))

    place, place_t, same_query, first, expand = call(
        maps_kernel,
        [
            ((slots, branches), BF16),
            ((branches, slots), BF16),
            ((branches, branches), BF16),
            ((queries, branches), BF16),
            ((branches, queries), BF16),
        ],
        10 * branches * slots,
        4 * branches * slots,
    )(rel_row, rel_ids, query_of, query_col)

    block = 256
    half = slots // 2
    columns = 896
    whole = lambda shape: pl.BlockSpec(shape, lambda i: (0, 0))
    rows_of = lambda cols: pl.BlockSpec((block, cols), lambda i: (i, 0))
    (moved,) = call(
        forward_kernel,
        [((slots, width), BF16)],
        4 * slots * width * hidden,
        4 * slots * width + 4 * width * hidden,
        limit=51,
        grid=(slots // half,),
        in_specs=[
            pl.BlockSpec((half, width), lambda i: (i, 0)),
            whole((width, hidden)),
            whole((width, hidden)),
        ],
        out_specs=[pl.BlockSpec((half, width), lambda i: (i, 0))],
    )(inputs, weight_in, weight_out_t)
    returned = exchange(moved)

    slope, inputs_t = call(
        slope_kernel,
        [((slots, hidden), BF16), ((width, slots), BF16)],
        2 * slots * width * hidden,
        2 * slots * hidden,
        grid=(slots // block,),
        in_specs=[rows_of(width), whole((width, hidden))],
        out_specs=[rows_of(hidden), pl.BlockSpec((width, block), lambda i: (0, i))],
    )(inputs, weight_in)

    returned, slope, inputs_t = lax.optimization_barrier((returned, slope, inputs_t))
    far = (returned, place_t, att_weight, same_query, first, cands, expand, place)
    outgoing, query_b = call(
        middle_kernel,
        [((slots, width), BF16), ((queries, width), BF16)],
        4 * branches * slots * width,
        8 * slots * width,
        in_specs=[NEAR] + [FAR] * len(far),
        out_specs=[NEAR] * 2,
        scratch_shapes=room(far),
    )(answer.reshape(queries, 1), *far)
    incoming = exchange(outgoing)

    loss, cand_part = call(
        loss_kernel,
        [((1, queries), F32), ((negatives, width), F32)],
        4 * queries * negatives * width,
        8 * negatives * width,
    )(cands, query_b, answer.reshape(1, queries))
    cand_grad = scatter_sum(cand_part, "ent")

    (w_in_grad,) = call(
        backward_kernel,
        [((width, hidden), BF16)],
        4 * slots * width * hidden,
        4 * slots * hidden,
        grid=(pl.cdiv(hidden, columns),),
        in_specs=[
            whole((slots, width)),
            pl.BlockSpec((width, columns), lambda i: (0, i)),
            pl.BlockSpec((slots, columns), lambda i: (0, i)),
            whole((width, slots)),
        ],
        out_specs=[pl.BlockSpec((width, columns), lambda i: (0, i))],
    )(incoming, weight_out_t, slope, inputs_t)
    return (loss.reshape(queries), cand_grad[None], w_in_grad[None])


def solution(mesh):
    placed = (
        P(BOTH, None),
        P(BOTH, None),
        P(BOTH, None),
        P(BOTH),
        P("rel", "ent"),
        P("ent", None),
        P(BOTH, None, None),
        P(BOTH, None, None),
        P(),
    )
    return jax.shard_map(
        shards,
        mesh=mesh,
        in_specs=placed,
        out_specs=(P(BOTH), P("rel", "ent", None), P(BOTH, None, None)),
        check_vma=False,
    )
```

```python
import jax
import jax.numpy as jnp
from jax import lax
from jax.experimental import pallas as pl
from jax.experimental.pallas import tpu as pltpu
from jax.sharding import PartitionSpec as P

GELU_C = 0.7978845608
GELU_K = 0.044715
ATT_GAIN = 3.0
BOTH = ("rel", "ent")
F32 = jnp.float32
BF16 = jnp.bfloat16
MIB = 1024 * 1024


def iota(shape, dim):
    return lax.broadcasted_iota(jnp.int32, shape, dim)


def mm(lhs, rhs, lhs_dim=1, rhs_dim=0):
    return lax.dot_general(
        lhs, rhs, (((lhs_dim,), (rhs_dim,)), ((), ())), preferred_element_type=F32
    )


def split(value):
    high = value.astype(BF16)
    return high, (value - high.astype(F32)).astype(BF16)


def call(kernel, outs, flops, moved, limit=56, **more):
    return pl.pallas_call(
        kernel,
        out_shape=[jax.ShapeDtypeStruct(shape, dtype) for shape, dtype in outs],
        compiler_params=pltpu.CompilerParams(vmem_limit_bytes=limit * MIB),
        cost_estimate=pl.CostEstimate(flops=flops, bytes_accessed=moved, transcendentals=0),
        **more,
    )


def fetch(sources, targets, sems):
    copies = [
        pltpu.make_async_copy(source, target, sems.at[number])
        for number, (source, target) in enumerate(zip(sources, targets))
    ]
    for copy in copies:
        copy.start()
    return copies


FAR = pl.BlockSpec(memory_space=pltpu.HBM)
NEAR = pl.BlockSpec(memory_space=pltpu.VMEM)


def room(arrays):
    return [pltpu.VMEM(a.shape, a.dtype) for a in arrays] + [
        pltpu.SemaphoreType.DMA((len(arrays),))
    ]


def paired(rows):
    return rows.reshape(rows.shape[0] // 2, 2, rows.shape[1])


def unpaired(pairs):
    return pairs.reshape(pairs.shape[0] * 2, pairs.shape[2])


def pack_kernel(rel_row, anchors_t, packed):
    count = rel_row.shape[1]
    row = rel_row[...]
    col = jnp.broadcast_to(row, (128, count)).T[:, :1]
    same = (col == row) & (iota((count, count), 0) < iota((count, count), 1))
    rank = jnp.sum(jnp.where(same, 1.0, 0.0), axis=0, keepdims=True).astype(jnp.int32)
    slot = row * 2 + rank
    rows = packed.shape[0] * 2
    step = 256
    for start in range(0, rows, step):
        hot = jnp.where(iota((step, count), 0) + start == slot, 1.0, 0.0).astype(BF16)
        part = mm(hot, anchors_t[...], 1, 1).astype(BF16)
        packed[start // 2 : (start + step) // 2] = paired(part)


def maps_kernel(
    rel_row, rel_col, query_row, query_col, place, place_t, same_query, first, expand
):
    count = rel_row.shape[1]
    queries = first.shape[0]
    col = rel_col[...]
    row = rel_row[...]
    below = iota((count, count), 0) < iota((count, count), 1)
    above = iota((count, count), 0) > iota((count, count), 1)
    equal = col == row
    rank = jnp.sum(jnp.where(equal & below, 1.0, 0.0), axis=0, keepdims=True)
    slot = row * 2 + rank.astype(jnp.int32)
    place[...] = jnp.where(iota(place.shape, 0) == slot, 1.0, 0.0).astype(BF16)
    rank = jnp.sum(jnp.where(equal & above, 1.0, 0.0), axis=1, keepdims=True)
    slot = col * 2 + rank.astype(jnp.int32)
    place_t[...] = jnp.where(iota(place_t.shape, 1) == slot, 1.0, 0.0).astype(BF16)
    q_row = query_row[...]
    q_col = query_col[...]
    together = q_row == q_col
    same_query[...] = jnp.where(together, 1.0, 0.0).astype(BF16)
    before = jnp.sum(jnp.where(together & below, 1.0, 0.0), axis=0, keepdims=True)
    leading = jnp.where(before == 0.0, q_row, -1)
    first[...] = jnp.where(iota((queries, count), 0) == leading, 1.0, 0.0).astype(BF16)
    expand[...] = jnp.where(iota((count, queries), 1) == q_col, 1.0, 0.0).astype(BF16)


def gelu(pre):
    tangent = jnp.tanh(GELU_C * (pre + GELU_K * pre * pre * pre))
    return 0.5 * pre * (1.0 + tangent)


def gelu_slope(pre):
    square = pre * pre
    tangent = jnp.tanh(GELU_C * (pre + GELU_K * pre * square))
    return 0.5 * (1.0 + tangent) + 0.5 * pre * (1.0 - tangent * tangent) * GELU_C * (
        1.0 + 3.0 * GELU_K * square
    )


def forward_kernel(inputs, w_in, w_out_t, moved):
    rows = unpaired(inputs[...])
    hidden = gelu(mm(rows, w_in[...])).astype(BF16)
    moved[...] = paired((rows.astype(F32) + mm(hidden, w_out_t[...], 1, 1)).astype(BF16))


def slope_kernel(inputs, w_in, slope, inputs_t):
    rows = unpaired(inputs[...])
    slope[...] = gelu_slope(mm(rows, w_in[...])).astype(BF16)
    inputs_t[...] = rows.T


def sigmoid_parts(scores, is_answer, negatives):
    signed = jnp.where(is_answer, -scores, scores)
    small = jnp.exp(-jnp.abs(signed))
    weight = jnp.where(is_answer, -1.0, 1.0 / (negatives - 1))
    sigmoid = jnp.where(signed >= 0.0, 1.0, small) / (1.0 + small)
    return signed, small, (sigmoid * weight).astype(BF16)


def middle_kernel(
    answer,
    far_returned,
    far_place_t,
    far_weight,
    far_same,
    far_first,
    far_cands,
    far_expand,
    far_place,
    outgoing,
    query_b,
    returned,
    place_t,
    att_weight,
    same_query,
    first,
    cands,
    expand,
    place,
    sems,
):
    copies = fetch(
        (
            far_returned,
            far_place_t,
            far_weight,
            far_same,
            far_first,
            far_cands,
            far_expand,
            far_place,
        ),
        (returned, place_t, att_weight, same_query, first, cands, expand, place),
        sems,
    )
    scale = returned.shape[2] ** (-0.5)
    copies[0].wait()
    copies[1].wait()
    projected = mm(place_t[...], unpaired(returned[...]))
    copies[2].wait()
    att_tanh = jnp.tanh(mm(projected.astype(BF16), att_weight[...]))
    att_exp = jnp.exp(ATT_GAIN * att_tanh)
    exp_hi, exp_lo = split(att_exp)
    both_hi, both_lo = split(att_exp * projected)
    copies[3].wait()
    group = same_query[...]
    inverse = 1.0 / (mm(group, exp_hi) + mm(group, exp_lo))
    query_each = (mm(group, both_hi) + mm(group, both_lo)) * inverse
    share = att_exp * inverse
    copies[4].wait()
    queries = mm(first[...], query_each.astype(BF16)).astype(BF16)
    query_b[...] = queries
    copies[5].wait()
    scores = mm(queries, cands[...], 1, 1) * scale
    is_answer = iota(scores.shape, 1) == answer[...]
    _, _, coefficient = sigmoid_parts(scores, is_answer, scores.shape[1])
    grad_hi, grad_lo = split(mm(coefficient, cands[...]) * scale)
    copies[6].wait()
    spread = expand[...]
    grad_each = (mm(spread, grad_hi) + mm(spread, grad_lo)) * share
    pre_grad = grad_each * (projected - query_each) * ATT_GAIN * (1.0 - att_tanh * att_tanh)
    proj_grad = grad_each + mm(pre_grad.astype(BF16), att_weight[...], 1, 1)
    copies[7].wait()
    outgoing[...] = paired(mm(place[...], proj_grad.astype(BF16)).astype(BF16))


def loss_kernel(cands, query_b, answer, loss, cand_part):
    negatives, width = cands.shape
    scale = width ** (-0.5)
    queries = query_b[...]
    scores = mm(cands[...], queries, 1, 1) * scale
    is_answer = iota(scores.shape, 0) == answer[...]
    signed, small, coefficient = sigmoid_parts(scores, is_answer, negatives)
    softplus = jnp.maximum(signed, 0.0) + jnp.log1p(small)
    weight = jnp.where(is_answer, 1.0, 1.0 / (negatives - 1))
    loss[...] = jnp.sum(softplus * weight, axis=0, keepdims=True)
    cand_part[...] = mm(coefficient, queries) * scale


def backward_kernel(incoming, w_out_t, slope, inputs_t, w_in_grad):
    part = (mm(unpaired(incoming[...]), w_out_t[...]) * slope[...].astype(F32)).astype(BF16)
    w_in_grad[...] = mm(inputs_t[...], part).astype(BF16)


def scatter_sum(part, axis):
    count = lax.axis_size(axis)
    me = lax.axis_index(axis)
    gap = count // 2
    while gap:
        half = part.shape[0] // 2
        low, high = part[:half], part[half:]
        upper = (me & gap) != 0
        sent = jnp.where(upper, low, high)
        kept = jnp.where(upper, high, low)
        pairs = [(i, i ^ gap) for i in range(count)]
        got = lax.ppermute(sent.astype(BF16), axis, pairs)
        part = kept + got.astype(F32)
        gap //= 2
    return part


def shards(anchors, rel_ids, query_of, answer, cand_ids, ent_table, w_in, w_out, att_weight):
    owners = lax.axis_size("rel") * lax.axis_size("ent")
    branches, width = anchors.shape
    queries = answer.shape[0]
    slots = 2 * owners
    hidden = w_in.shape[2]
    weight_in = w_in[0]
    weight_out_t = w_out[0].T

    def exchange(pairs):
        return lax.all_to_all(pairs, BOTH, split_axis=0, concat_axis=0, tiled=True)

    rel_row = rel_ids.reshape(1, branches)
    query_col = query_of.reshape(branches, 1)
    (packed,) = call(
        pack_kernel,
        [((owners, 2, width), BF16)],
        2 * slots * branches * width,
        4 * slots * branches,
        limit=16,
    )(rel_row, anchors.T)
    inputs = exchange(packed)

    local_ids = cand_ids[0] - lax.axis_index("ent") * ent_table.shape[0]
    chosen = (local_ids[:, None] == iota((local_ids.shape[0], ent_table.shape[0]), 1)).astype(BF16)
    picked = jnp.dot(chosen, ent_table, preferred_element_type=F32).astype(BF16)
    cands = lax.all_gather(picked, "ent", axis=0, tiled=True)
    negatives = cands.shape[0]
    inputs, cands = lax.optimization_barrier((inputs, cands))

    place, place_t, same_query, first, expand = call(
        maps_kernel,
        [
            ((slots, branches), BF16),
            ((branches, slots), BF16),
            ((branches, branches), BF16),
            ((queries, branches), BF16),
            ((branches, queries), BF16),
        ],
        10 * branches * slots,
        4 * branches * slots,
    )(rel_row, rel_ids, query_of, query_col)

    block = 256
    half = slots // 2
    columns = 896
    whole = lambda shape: pl.BlockSpec(shape, lambda i: (0, 0))
    pairs_of = lambda rows: pl.BlockSpec((rows // 2, 2, width), lambda i: (i, 0, 0))
    rows_of = lambda cols: pl.BlockSpec((block, cols), lambda i: (i, 0))
    (moved,) = call(
        forward_kernel,
        [((owners, 2, width), BF16)],
        4 * slots * width * hidden,
        4 * slots * width + 4 * width * hidden,
        limit=51,
        grid=(slots // half,),
        in_specs=[
            pairs_of(half),
            whole((width, hidden)),
            whole((width, hidden)),
        ],
        out_specs=[pairs_of(half)],
    )(inputs, weight_in, weight_out_t)
    returned = exchange(moved)

    slope, inputs_t = call(
        slope_kernel,
        [((slots, hidden), BF16), ((width, slots), BF16)],
        2 * slots * width * hidden,
        2 * slots * hidden,
        grid=(slots // block,),
        in_specs=[pairs_of(block), whole((width, hidden))],
        out_specs=[rows_of(hidden), pl.BlockSpec((width, block), lambda i: (0, i))],
    )(inputs, weight_in)

    returned, slope, inputs_t = lax.optimization_barrier((returned, slope, inputs_t))
    far = (returned, place_t, att_weight, same_query, first, cands, expand, place)
    outgoing, query_b = call(
        middle_kernel,
        [((owners, 2, width), BF16), ((queries, width), BF16)],
        4 * branches * slots * width,
        8 * slots * width,
        in_specs=[NEAR] + [FAR] * len(far),
        out_specs=[NEAR] * 2,
        scratch_shapes=room(far),
    )(answer.reshape(queries, 1), *far)
    incoming = exchange(outgoing)

    loss, cand_part = call(
        loss_kernel,
        [((1, queries), F32), ((negatives, width), F32)],
        4 * queries * negatives * width,
        8 * negatives * width,
    )(cands, query_b, answer.reshape(1, queries))
    cand_grad = scatter_sum(cand_part, "ent")

    (w_in_grad,) = call(
        backward_kernel,
        [((width, hidden), BF16)],
        4 * slots * width * hidden,
        4 * slots * hidden,
        limit=52,
        grid=(pl.cdiv(hidden, columns),),
        in_specs=[
            pl.BlockSpec((owners, 2, width), lambda i: (0, 0, 0)),
            pl.BlockSpec((width, columns), lambda i: (0, i)),
            pl.BlockSpec((slots, columns), lambda i: (0, i)),
            whole((width, slots)),
        ],
        out_specs=[pl.BlockSpec((width, columns), lambda i: (0, i))],
    )(incoming, weight_out_t, slope, inputs_t)
    return (loss.reshape(queries), cand_grad[None], w_in_grad[None])


def solution(mesh):
    placed = (
        P(BOTH, None),
        P(BOTH, None),
        P(BOTH, None),
        P(BOTH),
        P("rel", "ent"),
        P("ent", None),
        P(BOTH, None, None),
        P(BOTH, None, None),
        P(),
    )
    return jax.shard_map(
        shards,
        mesh=mesh,
        in_specs=placed,
        out_specs=(P(BOTH), P("rel", "ent", None), P(BOTH, None, None)),
        check_vma=False,
    )
```

```python
import jax
import jax.numpy as jnp
from jax import lax
from jax.experimental import pallas as pl
from jax.experimental.pallas import tpu as pltpu
from jax.sharding import PartitionSpec as P

GELU_C = 0.7978845608
GELU_K = 0.044715
ATT_GAIN = 3.0
BOTH = ("rel", "ent")
F32 = jnp.float32
BF16 = jnp.bfloat16
MIB = 1024 * 1024


def iota(shape, dim):
    return lax.broadcasted_iota(jnp.int32, shape, dim)


def mm(lhs, rhs, lhs_dim=1, rhs_dim=0):
    return lax.dot_general(
        lhs, rhs, (((lhs_dim,), (rhs_dim,)), ((), ())), preferred_element_type=F32
    )


def split(value):
    high = value.astype(BF16)
    return high, (value - high.astype(F32)).astype(BF16)


def call(kernel, outs, flops, moved, limit=56, **more):
    return pl.pallas_call(
        kernel,
        out_shape=[jax.ShapeDtypeStruct(shape, dtype) for shape, dtype in outs],
        compiler_params=pltpu.CompilerParams(vmem_limit_bytes=limit * MIB),
        cost_estimate=pl.CostEstimate(flops=flops, bytes_accessed=moved, transcendentals=0),
        **more,
    )


def fetch(sources, targets, sems):
    copies = [
        pltpu.make_async_copy(source, target, sems.at[number])
        for number, (source, target) in enumerate(zip(sources, targets))
    ]
    for copy in copies:
        copy.start()
    return copies


FAR = pl.BlockSpec(memory_space=pltpu.HBM)
NEAR = pl.BlockSpec(memory_space=pltpu.VMEM)


def room(arrays):
    return [pltpu.VMEM(a.shape, a.dtype) for a in arrays] + [
        pltpu.SemaphoreType.DMA((len(arrays),))
    ]


def paired(rows):
    return rows.reshape(rows.shape[0] // 2, 2, rows.shape[1])


def unpaired(pairs):
    return pairs.reshape(pairs.shape[0] * 2, pairs.shape[2])


def pack_kernel(rel_row, anchors_t, packed):
    count = rel_row.shape[1]
    row = rel_row[...]
    col = jnp.broadcast_to(row, (128, count)).T[:, :1]
    same = (col == row) & (iota((count, count), 0) < iota((count, count), 1))
    rank = jnp.sum(jnp.where(same, 1.0, 0.0), axis=0, keepdims=True).astype(jnp.int32)
    slot = row * 2 + rank
    rows = packed.shape[0] * 2
    step = 256
    for start in range(0, rows, step):
        hot = jnp.where(iota((step, count), 0) + start == slot, 1.0, 0.0).astype(BF16)
        part = mm(hot, anchors_t[...], 1, 1).astype(BF16)
        packed[start // 2 : (start + step) // 2] = paired(part)


def maps_kernel(
    rel_row, rel_col, query_row, query_col, place, place_t, same_query, first, expand
):
    count = rel_row.shape[1]
    queries = first.shape[0]
    col = rel_col[...]
    row = rel_row[...]
    below = iota((count, count), 0) < iota((count, count), 1)
    above = iota((count, count), 0) > iota((count, count), 1)
    equal = col == row
    rank = jnp.sum(jnp.where(equal & below, 1.0, 0.0), axis=0, keepdims=True)
    slot = row * 2 + rank.astype(jnp.int32)
    place[...] = jnp.where(iota(place.shape, 0) == slot, 1.0, 0.0).astype(BF16)
    rank = jnp.sum(jnp.where(equal & above, 1.0, 0.0), axis=1, keepdims=True)
    slot = col * 2 + rank.astype(jnp.int32)
    place_t[...] = jnp.where(iota(place_t.shape, 1) == slot, 1.0, 0.0).astype(BF16)
    q_row = query_row[...]
    q_col = query_col[...]
    together = q_row == q_col
    same_query[...] = jnp.where(together, 1.0, 0.0).astype(BF16)
    before = jnp.sum(jnp.where(together & below, 1.0, 0.0), axis=0, keepdims=True)
    leading = jnp.where(before == 0.0, q_row, -1)
    first[...] = jnp.where(iota((queries, count), 0) == leading, 1.0, 0.0).astype(BF16)
    expand[...] = jnp.where(iota((count, queries), 1) == q_col, 1.0, 0.0).astype(BF16)


def gelu(pre):
    tangent = jnp.tanh(GELU_C * (pre + GELU_K * pre * pre * pre))
    return 0.5 * pre * (1.0 + tangent)


def gelu_slope(pre):
    square = pre * pre
    tangent = jnp.tanh(GELU_C * (pre + GELU_K * pre * square))
    return 0.5 * (1.0 + tangent) + 0.5 * pre * (1.0 - tangent * tangent) * GELU_C * (
        1.0 + 3.0 * GELU_K * square
    )


def forward_kernel(inputs, w_in, w_out_t, moved):
    rows = unpaired(inputs[...])
    hidden = gelu(mm(rows, w_in[...])).astype(BF16)
    moved[...] = paired((rows.astype(F32) + mm(hidden, w_out_t[...], 1, 1)).astype(BF16))


def slope_kernel(inputs, w_in, slope, inputs_t):
    rows = unpaired(inputs[...])
    slope[...] = gelu_slope(mm(rows, w_in[...])).astype(BF16)
    inputs_t[...] = rows.T


def sigmoid_parts(scores, is_answer, negatives):
    signed = jnp.where(is_answer, -scores, scores)
    small = jnp.exp(-jnp.abs(signed))
    weight = jnp.where(is_answer, -1.0, 1.0 / (negatives - 1))
    sigmoid = jnp.where(signed >= 0.0, 1.0, small) / (1.0 + small)
    return signed, small, (sigmoid * weight).astype(BF16)


def middle_kernel(
    answer,
    far_returned,
    far_place_t,
    far_weight,
    far_same,
    far_first,
    far_cands,
    far_expand,
    far_place,
    outgoing,
    query_b,
    returned,
    place_t,
    att_weight,
    same_query,
    first,
    cands,
    expand,
    place,
    sems,
    ready,
    out_sems,
):
    copies = fetch(
        (
            far_returned,
            far_place_t,
            far_weight,
            far_same,
            far_first,
            far_cands,
            far_expand,
            far_place,
        ),
        (returned, place_t, att_weight, same_query, first, cands, expand, place),
        sems,
    )
    scale = returned.shape[2] ** (-0.5)
    copies[0].wait()
    copies[1].wait()
    projected = mm(place_t[...], unpaired(returned[...]))
    copies[2].wait()
    att_tanh = jnp.tanh(mm(projected.astype(BF16), att_weight[...]))
    att_exp = jnp.exp(ATT_GAIN * att_tanh)
    exp_hi, exp_lo = split(att_exp)
    both_hi, both_lo = split(att_exp * projected)
    copies[3].wait()
    group = same_query[...]
    inverse = 1.0 / (mm(group, exp_hi) + mm(group, exp_lo))
    query_each = (mm(group, both_hi) + mm(group, both_lo)) * inverse
    share = att_exp * inverse
    copies[4].wait()
    queries = mm(first[...], query_each.astype(BF16)).astype(BF16)
    query_b[...] = queries
    copies[5].wait()
    scores = mm(queries, cands[...], 1, 1) * scale
    is_answer = iota(scores.shape, 1) == answer[...]
    _, _, coefficient = sigmoid_parts(scores, is_answer, scores.shape[1])
    grad_hi, grad_lo = split(mm(coefficient, cands[...]) * scale)
    copies[6].wait()
    spread = expand[...]
    grad_each = (mm(spread, grad_hi) + mm(spread, grad_lo)) * share
    pre_grad = grad_each * (projected - query_each) * ATT_GAIN * (1.0 - att_tanh * att_tanh)
    proj_grad = grad_each + mm(pre_grad.astype(BF16), att_weight[...], 1, 1)
    copies[7].wait()
    grads = proj_grad.astype(BF16)
    pairs = ready.shape[0]
    leaving = []
    for number in range(4):
        part = slice(number * pairs // 4, (number + 1) * pairs // 4)
        rows = slice(number * pairs // 2, (number + 1) * pairs // 2)
        ready[part] = paired(mm(place[rows, :], grads).astype(BF16))
        copy = pltpu.make_async_copy(ready.at[part], outgoing.at[part], out_sems.at[number])
        copy.start()
        leaving.append(copy)
    for copy in leaving:
        copy.wait()


def loss_kernel(cands, query_b, answer, loss, cand_part):
    negatives, width = cands.shape
    scale = width ** (-0.5)
    queries = query_b[...]
    scores = mm(cands[...], queries, 1, 1) * scale
    is_answer = iota(scores.shape, 0) == answer[...]
    signed, small, coefficient = sigmoid_parts(scores, is_answer, negatives)
    softplus = jnp.maximum(signed, 0.0) + jnp.log1p(small)
    weight = jnp.where(is_answer, 1.0, 1.0 / (negatives - 1))
    loss[...] = jnp.sum(softplus * weight, axis=0, keepdims=True)
    cand_part[...] = mm(coefficient, queries) * scale


def backward_kernel(incoming, w_out_t, slope, inputs_t, w_in_grad):
    part = (mm(unpaired(incoming[...]), w_out_t[...]) * slope[...].astype(F32)).astype(BF16)
    w_in_grad[...] = mm(inputs_t[...], part).astype(BF16)


def scatter_sum(part, axis):
    count = lax.axis_size(axis)
    me = lax.axis_index(axis)
    gap = count // 2
    while gap:
        half = part.shape[0] // 2
        low, high = part[:half], part[half:]
        upper = (me & gap) != 0
        sent = jnp.where(upper, low, high)
        kept = jnp.where(upper, high, low)
        pairs = [(i, i ^ gap) for i in range(count)]
        got = lax.ppermute(sent.astype(BF16), axis, pairs)
        part = kept + got.astype(F32)
        gap //= 2
    return part


def shards(anchors, rel_ids, query_of, answer, cand_ids, ent_table, w_in, w_out, att_weight):
    owners = lax.axis_size("rel") * lax.axis_size("ent")
    branches, width = anchors.shape
    queries = answer.shape[0]
    slots = 2 * owners
    hidden = w_in.shape[2]
    weight_in = w_in[0]
    weight_out_t = w_out[0].T

    def exchange(pairs):
        return lax.all_to_all(pairs, BOTH, split_axis=0, concat_axis=0, tiled=True)

    rel_row = rel_ids.reshape(1, branches)
    query_col = query_of.reshape(branches, 1)
    (packed,) = call(
        pack_kernel,
        [((owners, 2, width), BF16)],
        2 * slots * branches * width,
        4 * slots * branches,
    )(rel_row, anchors.T)
    inputs = exchange(packed)

    local_ids = cand_ids[0] - lax.axis_index("ent") * ent_table.shape[0]
    chosen = (local_ids[:, None] == iota((local_ids.shape[0], ent_table.shape[0]), 1)).astype(BF16)
    picked = jnp.dot(chosen, ent_table, preferred_element_type=F32).astype(BF16)
    cands = lax.all_gather(picked, "ent", axis=0, tiled=True)
    negatives = cands.shape[0]
    inputs, cands = lax.optimization_barrier((inputs, cands))

    place, place_t, same_query, first, expand = call(
        maps_kernel,
        [
            ((slots, branches), BF16),
            ((branches, slots), BF16),
            ((branches, branches), BF16),
            ((queries, branches), BF16),
            ((branches, queries), BF16),
        ],
        10 * branches * slots,
        4 * branches * slots,
    )(rel_row, rel_ids, query_of, query_col)

    block = 256
    half = slots // 2
    columns = 896
    whole = lambda shape: pl.BlockSpec(shape, lambda i: (0, 0))
    pairs_of = lambda rows: pl.BlockSpec((rows // 2, 2, width), lambda i: (i, 0, 0))
    rows_of = lambda cols: pl.BlockSpec((block, cols), lambda i: (i, 0))
    (moved,) = call(
        forward_kernel,
        [((owners, 2, width), BF16)],
        4 * slots * width * hidden,
        4 * slots * width + 4 * width * hidden,
        limit=50,
        grid=(slots // half,),
        in_specs=[
            pairs_of(half),
            whole((width, hidden)),
            whole((width, hidden)),
        ],
        out_specs=[pairs_of(half)],
    )(inputs, weight_in, weight_out_t)
    returned = exchange(moved)

    slope, inputs_t = call(
        slope_kernel,
        [((slots, hidden), BF16), ((width, slots), BF16)],
        2 * slots * width * hidden,
        2 * slots * hidden,
        grid=(slots // block,),
        in_specs=[pairs_of(block), whole((width, hidden))],
        out_specs=[rows_of(hidden), pl.BlockSpec((width, block), lambda i: (0, i))],
    )(inputs, weight_in)

    returned, slope, inputs_t = lax.optimization_barrier((returned, slope, inputs_t))
    far = (returned, place_t, att_weight, same_query, first, cands, expand, place)
    outgoing, query_b = call(
        middle_kernel,
        [((owners, 2, width), BF16), ((queries, width), BF16)],
        4 * branches * slots * width,
        8 * slots * width,
        in_specs=[NEAR] + [FAR] * len(far),
        out_specs=[FAR, NEAR],
        scratch_shapes=room(far)
        + [pltpu.VMEM((owners, 2, width), BF16), pltpu.SemaphoreType.DMA((4,))],
    )(answer.reshape(queries, 1), *far)
    incoming = exchange(outgoing)

    loss, cand_part = call(
        loss_kernel,
        [((1, queries), F32), ((negatives, width), F32)],
        4 * queries * negatives * width,
        8 * negatives * width,
    )(cands, query_b, answer.reshape(1, queries))
    cand_grad = scatter_sum(cand_part, "ent")

    (w_in_grad,) = call(
        backward_kernel,
        [((width, hidden), BF16)],
        4 * slots * width * hidden,
        4 * slots * hidden,
        limit=52,
        grid=(pl.cdiv(hidden, columns),),
        in_specs=[
            pl.BlockSpec((owners, 2, width), lambda i: (0, 0, 0)),
            pl.BlockSpec((width, columns), lambda i: (0, i)),
            pl.BlockSpec((slots, columns), lambda i: (0, i)),
            whole((width, slots)),
        ],
        out_specs=[pl.BlockSpec((width, columns), lambda i: (0, i))],
    )(incoming, weight_out_t, slope, inputs_t)
    return (loss.reshape(queries), cand_grad[None], w_in_grad[None])


def solution(mesh):
    placed = (
        P(BOTH, None),
        P(BOTH, None),
        P(BOTH, None),
        P(BOTH),
        P("rel", "ent"),
        P("ent", None),
        P(BOTH, None, None),
        P(BOTH, None, None),
        P(),
    )
    return jax.shard_map(
        shards,
        mesh=mesh,
        in_specs=placed,
        out_specs=(P(BOTH), P("rel", "ent", None), P(BOTH, None, None)),
        check_vma=False,
    )
```

```python
import jax
import jax.numpy as jnp
from jax import lax
from jax.experimental import pallas as pl
from jax.experimental.pallas import tpu as pltpu
from jax.sharding import PartitionSpec as P

GELU_C = 0.7978845608
GELU_K = 0.044715
ATT_GAIN = 3.0
BOTH = ("rel", "ent")
F32 = jnp.float32
BF16 = jnp.bfloat16
MIB = 1024 * 1024


def iota(shape, dim):
    return lax.broadcasted_iota(jnp.int32, shape, dim)


def mm(lhs, rhs, lhs_dim=1, rhs_dim=0):
    return lax.dot_general(
        lhs, rhs, (((lhs_dim,), (rhs_dim,)), ((), ())), preferred_element_type=F32
    )


def split(value):
    high = value.astype(BF16)
    return high, (value - high.astype(F32)).astype(BF16)


def call(kernel, outs, flops, moved, limit=56, **more):
    return pl.pallas_call(
        kernel,
        out_shape=[jax.ShapeDtypeStruct(shape, dtype) for shape, dtype in outs],
        compiler_params=pltpu.CompilerParams(vmem_limit_bytes=limit * MIB),
        cost_estimate=pl.CostEstimate(flops=flops, bytes_accessed=moved, transcendentals=0),
        **more,
    )


def fetch(sources, targets, sems):
    copies = [
        pltpu.make_async_copy(source, target, sems.at[number])
        for number, (source, target) in enumerate(zip(sources, targets))
    ]
    for copy in copies:
        copy.start()
    return copies


FAR = pl.BlockSpec(memory_space=pltpu.HBM)
NEAR = pl.BlockSpec(memory_space=pltpu.VMEM)


def room(arrays):
    return [pltpu.VMEM(a.shape, a.dtype) for a in arrays] + [
        pltpu.SemaphoreType.DMA((len(arrays),))
    ]


def paired(rows):
    return rows.reshape(rows.shape[0] // 2, 2, rows.shape[1])


def unpaired(pairs):
    return pairs.reshape(pairs.shape[0] * 2, pairs.shape[2])


def pack_kernel(rel_row, anchors_t, packed):
    count = rel_row.shape[1]
    row = rel_row[...]
    col = jnp.broadcast_to(row, (128, count)).T[:, :1]
    same = (col == row) & (iota((count, count), 0) < iota((count, count), 1))
    rank = jnp.sum(jnp.where(same, 1.0, 0.0), axis=0, keepdims=True).astype(jnp.int32)
    slot = row * 2 + rank
    rows = packed.shape[0] * 2
    step = 256
    for start in range(0, rows, step):
        hot = jnp.where(iota((step, count), 0) + start == slot, 1.0, 0.0).astype(BF16)
        part = mm(hot, anchors_t[...], 1, 1).astype(BF16)
        packed[start // 2 : (start + step) // 2] = paired(part)


def maps_kernel(
    rel_row, rel_col, query_row, query_col, place, place_t, same_query, first, expand
):
    count = rel_row.shape[1]
    queries = first.shape[0]
    col = rel_col[...]
    row = rel_row[...]
    below = iota((count, count), 0) < iota((count, count), 1)
    above = iota((count, count), 0) > iota((count, count), 1)
    equal = col == row
    rank = jnp.sum(jnp.where(equal & below, 1.0, 0.0), axis=0, keepdims=True)
    slot = row * 2 + rank.astype(jnp.int32)
    place[...] = jnp.where(iota(place.shape, 0) == slot, 1.0, 0.0).astype(BF16)
    rank = jnp.sum(jnp.where(equal & above, 1.0, 0.0), axis=1, keepdims=True)
    slot = col * 2 + rank.astype(jnp.int32)
    place_t[...] = jnp.where(iota(place_t.shape, 1) == slot, 1.0, 0.0).astype(BF16)
    q_row = query_row[...]
    q_col = query_col[...]
    together = q_row == q_col
    same_query[...] = jnp.where(together, 1.0, 0.0).astype(BF16)
    before = jnp.sum(jnp.where(together & below, 1.0, 0.0), axis=0, keepdims=True)
    leading = jnp.where(before == 0.0, q_row, -1)
    first[...] = jnp.where(iota((queries, count), 0) == leading, 1.0, 0.0).astype(BF16)
    expand[...] = jnp.where(iota((count, queries), 1) == q_col, 1.0, 0.0).astype(BF16)


def gelu(pre):
    tangent = jnp.tanh(GELU_C * (pre + GELU_K * pre * pre * pre))
    return 0.5 * pre * (1.0 + tangent)


def gelu_slope(pre):
    square = pre * pre
    tangent = jnp.tanh(GELU_C * (pre + GELU_K * pre * square))
    return 0.5 * (1.0 + tangent) + 0.5 * pre * (1.0 - tangent * tangent) * GELU_C * (
        1.0 + 3.0 * GELU_K * square
    )


def forward_kernel(inputs, w_in, w_out_t, moved):
    rows = unpaired(inputs[...])
    hidden = gelu(mm(rows, w_in[...])).astype(BF16)
    moved[...] = paired((rows.astype(F32) + mm(hidden, w_out_t[...], 1, 1)).astype(BF16))


def slope_kernel(inputs, w_in, slope, inputs_t):
    rows = unpaired(inputs[...])
    slope[...] = gelu_slope(mm(rows, w_in[...])).astype(BF16)
    inputs_t[...] = rows.T


def sigmoid_parts(scores, is_answer, negatives):
    signed = jnp.where(is_answer, -scores, scores)
    small = jnp.exp(-jnp.abs(signed))
    weight = jnp.where(is_answer, -1.0, 1.0 / (negatives - 1))
    sigmoid = jnp.where(signed >= 0.0, 1.0, small) / (1.0 + small)
    return signed, small, (sigmoid * weight).astype(BF16)


def middle_kernel(
    answer,
    far_returned,
    far_place_t,
    far_weight,
    far_same,
    far_first,
    far_cands,
    far_expand,
    far_place,
    outgoing,
    query_b,
    returned,
    place_t,
    att_weight,
    same_query,
    first,
    cands,
    expand,
    place,
    sems,
    ready,
    out_sems,
):
    copies = fetch(
        (
            far_returned,
            far_place_t,
            far_weight,
            far_same,
            far_first,
            far_cands,
            far_expand,
            far_place,
        ),
        (returned, place_t, att_weight, same_query, first, cands, expand, place),
        sems,
    )
    scale = returned.shape[2] ** (-0.5)
    copies[0].wait()
    copies[1].wait()
    projected = mm(place_t[...], unpaired(returned[...]))
    copies[2].wait()
    att_tanh = jnp.tanh(mm(projected.astype(BF16), att_weight[...]))
    att_exp = jnp.exp(ATT_GAIN * att_tanh)
    exp_hi, exp_lo = split(att_exp)
    both_hi, both_lo = split(att_exp * projected)
    copies[3].wait()
    group = same_query[...]
    inverse = 1.0 / (mm(group, exp_hi) + mm(group, exp_lo))
    query_each = (mm(group, both_hi) + mm(group, both_lo)) * inverse
    share = att_exp * inverse
    copies[4].wait()
    queries = mm(first[...], query_each.astype(BF16)).astype(BF16)
    query_b[...] = queries
    copies[5].wait()
    scores = mm(queries, cands[...], 1, 1) * scale
    is_answer = iota(scores.shape, 1) == answer[...]
    _, _, coefficient = sigmoid_parts(scores, is_answer, scores.shape[1])
    grad_hi, grad_lo = split(mm(coefficient, cands[...]) * scale)
    copies[6].wait()
    spread = expand[...]
    grad_each = (mm(spread, grad_hi) + mm(spread, grad_lo)) * share
    pre_grad = grad_each * (projected - query_each) * ATT_GAIN * (1.0 - att_tanh * att_tanh)
    proj_grad = grad_each + mm(pre_grad.astype(BF16), att_weight[...], 1, 1)
    copies[7].wait()
    grads = proj_grad.astype(BF16)
    pairs = ready.shape[0]
    leaving = []
    for number in range(4):
        part = slice(number * pairs // 4, (number + 1) * pairs // 4)
        rows = slice(number * pairs // 2, (number + 1) * pairs // 2)
        ready[part] = paired(mm(place[rows, :], grads).astype(BF16))
        copy = pltpu.make_async_copy(ready.at[part], outgoing.at[part], out_sems.at[number])
        copy.start()
        leaving.append(copy)
    for copy in leaving:
        copy.wait()


def scores_by_candidate(cands, queries, answer):
    scores = mm(cands[...], queries, 1, 1) * cands.shape[1] ** (-0.5)
    return scores, iota(scores.shape, 0) == answer[...]


def cand_kernel(cands, query_b, answer, cand_part):
    queries = query_b[...]
    scores, is_answer = scores_by_candidate(cands, queries, answer)
    _, _, coefficient = sigmoid_parts(scores, is_answer, cands.shape[0])
    cand_part[...] = mm(coefficient, queries) * cands.shape[1] ** (-0.5)


def loss_kernel(cands, query_b, answer, loss):
    scores, is_answer = scores_by_candidate(cands, query_b[...], answer)
    signed = jnp.where(is_answer, -scores, scores)
    softplus = jnp.maximum(signed, 0.0) + jnp.log1p(jnp.exp(-jnp.abs(signed)))
    weight = jnp.where(is_answer, 1.0, 1.0 / (cands.shape[0] - 1))
    loss[...] = jnp.sum(softplus * weight, axis=0, keepdims=True)


def backward_kernel(incoming, w_out_t, slope, inputs_t, w_in_grad):
    part = (mm(unpaired(incoming[...]), w_out_t[...]) * slope[...].astype(F32)).astype(BF16)
    w_in_grad[...] = mm(inputs_t[...], part).astype(BF16)


def scatter_sum(part, axis):
    count = lax.axis_size(axis)
    me = lax.axis_index(axis)
    gaps = [1 << bit for bit in range(count.bit_length() - 1)][::-1]
    part = part.reshape((2,) * len(gaps) + (part.shape[0] // count, part.shape[1]))
    for gap in sorted(gaps, key=lambda gap: (gap in gaps[::2], gap)):
        place = gaps.index(gap)
        low = lax.index_in_dim(part, 0, place, keepdims=False)
        high = lax.index_in_dim(part, 1, place, keepdims=False)
        upper = (me & gap) != 0
        sent = jnp.where(upper, low, high)
        kept = jnp.where(upper, high, low)
        pairs = [(i, i ^ gap) for i in range(count)]
        got = lax.ppermute(sent.astype(BF16), axis, pairs)
        part = kept + got.astype(F32)
        gaps.remove(gap)
    return part


def shards(anchors, rel_ids, query_of, answer, cand_ids, ent_table, w_in, w_out, att_weight):
    owners = lax.axis_size("rel") * lax.axis_size("ent")
    branches, width = anchors.shape
    queries = answer.shape[0]
    slots = 2 * owners
    hidden = w_in.shape[2]
    weight_in = w_in[0]
    weight_out_t = w_out[0].T

    def exchange(pairs):
        return lax.all_to_all(pairs, BOTH, split_axis=0, concat_axis=0, tiled=True)

    rel_row = rel_ids.reshape(1, branches)
    query_col = query_of.reshape(branches, 1)
    (packed,) = call(
        pack_kernel,
        [((owners, 2, width), BF16)],
        2 * slots * branches * width,
        4 * slots * branches,
    )(rel_row, anchors.T)
    inputs = exchange(packed)

    local_ids = cand_ids[0] - lax.axis_index("ent") * ent_table.shape[0]
    chosen = (local_ids[:, None] == iota((local_ids.shape[0], ent_table.shape[0]), 1)).astype(BF16)
    picked = jnp.dot(chosen, ent_table, preferred_element_type=F32).astype(BF16)
    cands = lax.all_gather(picked, "ent", axis=0, tiled=True)
    negatives = cands.shape[0]
    inputs, cands = lax.optimization_barrier((inputs, cands))

    place, place_t, same_query, first, expand = call(
        maps_kernel,
        [
            ((slots, branches), BF16),
            ((branches, slots), BF16),
            ((branches, branches), BF16),
            ((queries, branches), BF16),
            ((branches, queries), BF16),
        ],
        10 * branches * slots,
        4 * branches * slots,
    )(rel_row, rel_ids, query_of, query_col)

    block = 256
    half = slots // 2
    columns = 896
    whole = lambda shape: pl.BlockSpec(shape, lambda i: (0, 0))
    pairs_of = lambda rows: pl.BlockSpec((rows // 2, 2, width), lambda i: (i, 0, 0))
    rows_of = lambda cols: pl.BlockSpec((block, cols), lambda i: (i, 0))
    (moved,) = call(
        forward_kernel,
        [((owners, 2, width), BF16)],
        4 * slots * width * hidden,
        4 * slots * width + 4 * width * hidden,
        limit=50,
        grid=(slots // half,),
        in_specs=[
            pairs_of(half),
            whole((width, hidden)),
            whole((width, hidden)),
        ],
        out_specs=[pairs_of(half)],
    )(inputs, weight_in, weight_out_t)
    returned = exchange(moved)

    slope, inputs_t = call(
        slope_kernel,
        [((slots, hidden), BF16), ((width, slots), BF16)],
        2 * slots * width * hidden,
        2 * slots * hidden,
        grid=(slots // block,),
        in_specs=[pairs_of(block), whole((width, hidden))],
        out_specs=[rows_of(hidden), pl.BlockSpec((width, block), lambda i: (0, i))],
    )(inputs, weight_in)

    returned, slope, inputs_t = lax.optimization_barrier((returned, slope, inputs_t))
    far = (returned, place_t, att_weight, same_query, first, cands, expand, place)
    outgoing, query_b = call(
        middle_kernel,
        [((owners, 2, width), BF16), ((queries, width), BF16)],
        4 * branches * slots * width,
        8 * slots * width,
        in_specs=[NEAR] + [FAR] * len(far),
        out_specs=[FAR, NEAR],
        scratch_shapes=room(far)
        + [pltpu.VMEM((owners, 2, width), BF16), pltpu.SemaphoreType.DMA((4,))],
    )(answer.reshape(queries, 1), *far)
    incoming = exchange(outgoing)

    scored = (cands, query_b, answer.reshape(1, queries))
    (cand_part,) = call(
        cand_kernel,
        [((negatives, width), F32)],
        4 * queries * negatives * width,
        8 * negatives * width,
    )(*scored)
    (loss,) = call(
        loss_kernel,
        [((1, queries), F32)],
        2 * queries * negatives * width,
        2 * negatives * width,
    )(*scored)
    cand_grad = scatter_sum(cand_part, "ent")

    (w_in_grad,) = call(
        backward_kernel,
        [((width, hidden), BF16)],
        4 * slots * width * hidden,
        4 * slots * hidden,
        limit=52,
        grid=(pl.cdiv(hidden, columns),),
        in_specs=[
            pl.BlockSpec((owners, 2, width), lambda i: (0, 0, 0)),
            pl.BlockSpec((width, columns), lambda i: (0, i)),
            pl.BlockSpec((slots, columns), lambda i: (0, i)),
            whole((width, slots)),
        ],
        out_specs=[pl.BlockSpec((width, columns), lambda i: (0, i))],
    )(incoming, weight_out_t, slope, inputs_t)
    return (loss.reshape(queries), cand_grad[None], w_in_grad[None])


def solution(mesh):
    placed = (
        P(BOTH, None),
        P(BOTH, None),
        P(BOTH, None),
        P(BOTH),
        P("rel", "ent"),
        P("ent", None),
        P(BOTH, None, None),
        P(BOTH, None, None),
        P(),
    )
    return jax.shard_map(
        shards,
        mesh=mesh,
        in_specs=placed,
        out_specs=(P(BOTH), P("rel", "ent", None), P(BOTH, None, None)),
        check_vma=False,
    )
```
